32 devices in a mesh: groups: 2 (over y), side: 4 (over x, core), tp: 4 (over z).
Axes of the slice: x: 2, y: 2, z: 4, core: 2. Of those that a mesh axis runs over, the one named last changes fastest.
Arguments:
- tokens: bfloat16 [128, 6144], P(('groups', 'side', 'tp')), parts along dimension 0, may hold values from -6 to 6
- queries: bfloat16 [128, 6144], P(('groups', 'side', 'tp')), parts along dimension 0, may hold values from -120 to 120
- stored_keys: bfloat16 [128, 128, 1024], P(('groups', 'side', 'tp')), parts along dimension 0, may hold values from -4 to 4
- stored_values: bfloat16 [128, 128, 1024], P(('groups', 'side', 'tp')), parts along dimension 0, may hold values from -6 to 6
- lengths: int32 [128], P(('groups', 'side', 'tp')), parts along dimension 0, may hold values from 2 to 128, as said below
- norm_gain: float32 [6144], replicated, may hold values from 0.1 to 1.9
- routes: int32 [128, 2], P(('groups', 'side', 'tp')), parts along dimension 0, may hold values from 0 to 3, all different within a row; in each aligned block of 2 rows (0 to 1, 2 to 3, ...) at most 2 rows name the same one
- route_weights: float32 [128, 2], P(('groups', 'side', 'tp')), parts along dimension 0, may hold values from 0.2 to 1
- gate_up: bfloat16 [4, 2, 5376, 6144], P('side', None, 'tp'), may hold values from -0.078125 to 0.078125
- down_proj: bfloat16 [4, 5376, 6144], P('side', 'tp'), may hold values from -0.078125 to 0.078125
Outputs:
- mixed: bfloat16 [128, 6144], P(('groups', 'side', 'tp')), parts along dimension 0
The draws below stay inside these ranges and needn't reach their ends.
There are 2 independent parts, one for each index of `groups`. The reference program is written for one: setup_inputs(seed, part) draws one part's arguments, and reference() takes and returns one part's arrays. A program takes and returns all parts, laid end to end along the dimension named above; an argument that names none is the same for every part. Nothing has to cross between parts.
Inputs may be any that keep to these rules, and one draw needn't show every extreme that they name: `routes`: each row names 2 different experts; in each aligned block of 2 rows no expert is named by more than 2 rows, and in some blocks one is named by exactly 2. `lengths`: some sequences use all 128 positions.
All inputs are finite; a program needn't handle non-finite values.
Results may differ from the reference program's by a relative error of at most 0.0051.
Values may be sent and summed in bfloat16 or wider, within the bound.
No kernel may reach another device: no remote copies, remote signals or barrier semaphores. Data moves between devices by JAX's collectives and lax.ppermute only.
A program may use at most 128 MiB of HBM per device.

```python
import math
import jax
import jax.numpy as jnp
import numpy as np
from jax import lax

D = 6144
QUERY_HEADS = 48
KEY_VALUE_HEADS = 8
HEAD_SIZE = 128
FF = 5376
TOPK = 2
CACHE_LENGTH = 128
MB_DEV = 2
CAP = 2
EXPERTS = 4
SEQUENCE_COUNT = 64
N_TP = 4


def first_keys(key):
    return jnp.clip(jax.random.normal(key, (SEQUENCE_COUNT, KEY_VALUE_HEADS * HEAD_SIZE), jnp.float32), -4.0, 4.0)


def draw_stored_keys(key, part):
    leading_part = first_keys(key)
    key = jax.random.fold_in(key, 11)
    remaining_parts = jnp.clip(jax.random.normal(key, (SEQUENCE_COUNT, CACHE_LENGTH, KEY_VALUE_HEADS * HEAD_SIZE), jnp.float32), -4.0, 4.0)
    second = remaining_parts[:, 1]
    joined = jnp.concatenate([leading_part[:, None, :], second[:, None, :], remaining_parts[:, 2:, :]], axis=1)
    return joined.astype(jnp.bfloat16)


def draw_queries(key, part):
    key = jax.random.fold_in(key, 13)
    values = jnp.clip(jax.random.normal(key, (SEQUENCE_COUNT, QUERY_HEADS, HEAD_SIZE), jnp.float32), -4.0, 4.0)
    return values.reshape(SEQUENCE_COUNT, QUERY_HEADS * HEAD_SIZE).astype(jnp.bfloat16)


def draw_lengths(key, part):
    key = jax.random.fold_in(key, 17)
    values = jax.random.randint(key, (SEQUENCE_COUNT,), 2, CACHE_LENGTH + 1, dtype=jnp.int32)
    return jnp.where(jnp.arange(SEQUENCE_COUNT) % 4 == 0, CACHE_LENGTH, values).astype(jnp.int32)


def shard_levels(stream_key, extent, split, least, high):
    def one(axis_at, blocks):
        draws = jax.random.uniform(jax.random.fold_in(jax.random.fold_in(stream_key, 6), axis_at), (blocks,), jnp.float32, least / len(split), high / len(split))
        return jnp.repeat(jnp.exp(draws), extent[axis_at] // blocks).reshape((-1,) + (1,) * (len(extent) - axis_at - 1))

    level = one(*split[0])
    for cut in split[1:]:
        level = level * one(*cut)
    return level


def routed_block(key, own, number, rows, count, top, reach, lean):
    ranking = jax.random.permutation(key, count)
    crowded, common = shares(count, rows * top, reach, lean, True), shares(count, rows * top, reach, lean, False)
    places = jnp.arange(count)

    def named(sizes, turn):
        used = int((sizes > 0).sum())
        fixed = max(1, used // 4)
        shifted = fixed + (places - fixed + turn * (used - fixed)) % max(1, count - fixed)
        return jnp.zeros((count,), jnp.int32).at[ranking[jnp.where(places < fixed, places, shifted)]].set(jnp.asarray(sizes, jnp.int32))

    sizes = jnp.where(number % 4 == 0, named(crowded, number // 4), named(common, number - number // 4 - 1))
    mixed = jax.random.permutation(jax.random.fold_in(own, 3), count)
    giver, sink = mixed[0:count // 2 * 2:2], mixed[1:count // 2 * 2:2]
    room = jnp.minimum(sizes[giver] - 1, reach - sizes[sink]) // 2
    room = jnp.where((giver == ranking[0]) | (sink == ranking[0]) | (sizes[sink] == 0), 0, jnp.maximum(room, 0))
    shifted = jax.random.randint(jax.random.fold_in(own, 4), (count // 2,), 0, 1 << 20) % (room + 1)
    sizes = sizes.at[giver].add(-shifted).at[sink].add(shifted)
    members = jnp.searchsorted(jnp.cumsum(sizes), jnp.arange(rows * top), side="right").astype(jnp.int32)
    listing = members.reshape(top, rows).T
    listing = listing[jax.random.permutation(jax.random.fold_in(own, 1), rows)]
    turn = jax.random.randint(jax.random.fold_in(own, 2), (rows, 1), 0, top)
    return jnp.take_along_axis(listing, (jnp.arange(top)[None, :] + turn) % top, axis=1)


def shares(count, total, most, lean, full):
    portions = [(1 << 20) // math.isqrt(rank ** lean) + 1 for rank in range(1, count + 1)]
    largest = most if full else min(most, max(-(-total // count), total * portions[0] // sum(portions)))
    least = 1 if total - largest >= count - 1 else 0
    holding, surplus = [largest] + [least] * (count - 1), total - largest - least * (count - 1)
    while surplus > 0:
        candidates = [i for i in range(1, count) if holding[i] < largest] or [i for i in range(1, count) if holding[i] < most]
        whole, remaining = sum([portions[i] for i in candidates]), surplus
        for i in candidates:
            more = min(most - holding[i], max(1, remaining * portions[i] // whole), surplus)
            holding[i] = holding[i] + more
            surplus = surplus - more
    return np.array(holding)


def centred(rng, dims, spread, most, cuts=(), held_as=jnp.bfloat16):
    entries = spread * jax.random.normal(rng, dims, jnp.float32)
    if cuts:
        entries = entries * shard_levels(rng, dims, cuts, -0.22, 0.18)
    return jnp.clip(entries, -most, most).astype(held_as)


def setup_inputs(seed: int = 0, part: int = 0) -> dict:
    arg_keys = jax.random.split(jax.random.key(seed), 11)
    part_keys = jax.random.split(jax.random.fold_in(arg_keys[10], part), 11)
    tokens = centred(part_keys[0], (SEQUENCE_COUNT, D), 1.0, 6.0, ((0, 16),))
    queries = draw_queries(jax.random.fold_in(jax.random.fold_in(arg_keys[10], part), 71), part)
    stored_keys = draw_stored_keys(jax.random.fold_in(jax.random.fold_in(arg_keys[10], part), 71), part)
    stored_values = centred(part_keys[3], (SEQUENCE_COUNT, CACHE_LENGTH, KEY_VALUE_HEADS * HEAD_SIZE), 1.0, 6.0, ((0, 16),))
    lengths = draw_lengths(jax.random.fold_in(jax.random.fold_in(arg_keys[10], part), 71), part)
    norm_gain = jnp.clip(1.0 + 0.18 * jax.random.normal(arg_keys[5], (D,), jnp.float32), 0.1, 1.9)
    routes_keys = jax.random.split(jax.random.fold_in(part_keys[6], 1), SEQUENCE_COUNT // MB_DEV)
    routes_turns = jax.random.permutation(jax.random.fold_in(part_keys[6], 3), SEQUENCE_COUNT // MB_DEV)
    routes = jax.vmap(lambda own, number: routed_block(jax.random.fold_in(part_keys[6], 2), own, number, MB_DEV, EXPERTS, TOPK, CAP, 2))(routes_keys, routes_turns).reshape((SEQUENCE_COUNT, TOPK))
    route_weights = jnp.clip(0.2 + 0.8 * jax.random.uniform(part_keys[7], (SEQUENCE_COUNT, TOPK), jnp.float32) ** shard_levels(part_keys[7], (SEQUENCE_COUNT, TOPK), ((0, 16),), -0.2, 0.2), 0.2, 1.0)
    gate_up = centred(arg_keys[8], (EXPERTS, 2, FF, D), D ** -0.5, 0.078125, ((0, 4), (2, 4)))
    down_proj = centred(arg_keys[9], (EXPERTS, FF, D), FF ** -0.5, 0.078125, ((0, 4), (1, 4)))
    return dict(tokens=tokens, queries=queries, stored_keys=stored_keys, stored_values=stored_values, lengths=lengths, norm_gain=norm_gain, routes=routes, route_weights=route_weights, gate_up=gate_up, down_proj=down_proj)


def attend_norm(tokens, queries, stored_keys, stored_values, lengths, norm_gain):
    local_rows = tokens.shape[0]
    cache_positions = stored_keys.shape[1]
    query_head_rows = queries.astype(jnp.float32).reshape(local_rows, KEY_VALUE_HEADS, QUERY_HEADS // KEY_VALUE_HEADS, HEAD_SIZE)
    key_head_rows = stored_keys.astype(jnp.float32).reshape(local_rows, cache_positions, KEY_VALUE_HEADS, HEAD_SIZE)
    value_head_rows = stored_values.astype(jnp.float32).reshape(local_rows, cache_positions, KEY_VALUE_HEADS, HEAD_SIZE)
    scores = jnp.einsum('tkgd,tlkd->tkgl', query_head_rows, key_head_rows) / math.sqrt(HEAD_SIZE)
    alive_mask = (jnp.arange(cache_positions)[None, :] < lengths[:, None])[:, None, None, :]
    scores = jnp.where(alive_mask, scores, jnp.float32(-1e+30))
    peak = lax.optimization_barrier(jnp.max(scores, axis=-1, keepdims=True))
    expo = jnp.where(alive_mask, jnp.exp(scores - peak), jnp.float32(0.0))
    probabilities = (expo / lax.optimization_barrier(jnp.sum(expo, axis=-1, keepdims=True))).astype(jnp.bfloat16)
    attended = jnp.einsum('tkgl,tlkd->tkgd', probabilities.astype(jnp.float32), value_head_rows)
    resid = tokens.astype(jnp.float32) + attended.reshape(local_rows, QUERY_HEADS * HEAD_SIZE)
    scale = lax.rsqrt(lax.optimization_barrier(jnp.mean(resid * resid, axis=-1, keepdims=True)) + 1e-05)
    normed = (resid * scale * norm_gain[None, :]).astype(jnp.bfloat16)
    return (resid, normed)

def slot_numbers(routes, block_rows):
    flat_routes = routes.reshape(-1, block_rows * routes.shape[1])
    onehot = (flat_routes[:, :, None] == jnp.arange(EXPERTS, dtype=jnp.int32)[None, None, :]).astype(jnp.int32)
    before = jnp.cumsum(onehot, axis=1) - onehot
    return lax.optimization_barrier(jnp.sum(before * onehot, axis=-1)).astype(jnp.int32).reshape(routes.shape)

def expert_apply(buffer, weights_gu, weights_down):
    gate_proj = jnp.dot(buffer, weights_gu[0].T, preferred_element_type=jnp.float32)
    up_proj = jnp.dot(buffer, weights_gu[1].T, preferred_element_type=jnp.float32)
    hidden = (jax.nn.silu(gate_proj) * up_proj).astype(jnp.bfloat16)
    width = hidden.shape[1] // N_TP
    hidden_blocks = hidden.reshape(hidden.shape[0], N_TP, width).transpose(1, 0, 2)
    down_blocks = weights_down.reshape(N_TP, width, weights_down.shape[1])

    def add_block(total, pair):
        partial_value = jnp.dot(pair[0], pair[1], preferred_element_type=jnp.float32)
        partial_value = lax.optimization_barrier(partial_value.astype(jnp.bfloat16)).astype(jnp.float32)
        return (total + partial_value, None)
    start_total = jnp.zeros((buffer.shape[0], weights_down.shape[1]), jnp.float32)
    total, unused = lax.scan(add_block, start_total, (hidden_blocks, down_blocks))
    return total.astype(jnp.bfloat16)

def reference(tokens, queries, stored_keys, stored_values, lengths, norm_gain, routes, route_weights, gate_up, down_proj):
    resid, normed = attend_norm(tokens, queries, stored_keys, stored_values, lengths, norm_gain)
    slot_index = slot_numbers(routes, MB_DEV)
    blocks = SEQUENCE_COUNT // MB_DEV
    block_index = (jnp.arange(SEQUENCE_COUNT, dtype=jnp.int32) // MB_DEV).astype(jnp.int32)
    global_slot = (block_index[:, None] * CAP + slot_index).astype(jnp.int32)
    buffer = jnp.zeros((EXPERTS, blocks * CAP, D), jnp.bfloat16)
    spread_rows = jnp.broadcast_to(normed[:, None, :], (SEQUENCE_COUNT, TOPK, D))
    buffer = buffer.at[routes, global_slot].set(spread_rows)
    outputs = lax.map(lambda triple: expert_apply(triple[0], triple[1], triple[2]), (buffer, gate_up, down_proj))
    picked_rows = outputs[routes, global_slot].astype(jnp.float32)
    mixed = resid + lax.optimization_barrier(jnp.sum(route_weights[:, :, None] * picked_rows, axis=1))
    return mixed.astype(jnp.bfloat16)
```

```python
import functools
import math

import jax
import jax.numpy as jnp
from jax import lax
from jax.experimental import pallas as pl
from jax.experimental.pallas import tpu as pltpu
from jax.sharding import PartitionSpec as P

HEAD_SIZE = 128
LANES = 128
F32 = jnp.float32
BF16 = jnp.bfloat16


def attend_kernel(
    lengths, routes, weights, tokens, queries, gain, keys_hbm, values_hbm,
    resid_ref, row_ref, keys, values, key_sems, value_sems,
):
    rows, positions, kv_width = keys_hbm.shape
    width = tokens.shape[1]
    n_kv = kv_width // HEAD_SIZE
    per = width // kv_width
    key_copies = [
        pltpu.make_async_copy(keys_hbm.at[t], keys.at[t], key_sems.at[t]) for t in range(rows)
    ]
    value_copies = [
        pltpu.make_async_copy(values_hbm.at[t], values.at[t], value_sems.at[t])
        for t in range(rows)
    ]
    for copy in key_copies + value_copies:
        copy.start()
    block = per * rows
    owner = lax.broadcasted_iota(jnp.int32, (block, 1), 0) % rows
    length = jnp.zeros((block, 1), jnp.int32)
    for t in range(rows):
        length = jnp.where(owner == t, lengths[t], length)
    alive = lax.broadcasted_iota(jnp.int32, (block, positions), 1) < length
    q = queries[...].astype(F32)
    stacked = []
    for g in range(n_kv):
        heads = [
            q[:, (g * per + j) * HEAD_SIZE : (g * per + j + 1) * HEAD_SIZE] for j in range(per)
        ]
        stacked.append(jnp.concatenate(heads, axis=0))
    for copy in key_copies:
        copy.wait()
    scores = []
    for g in range(n_kv):
        total = jnp.zeros((block, positions), F32)
        for t in range(rows):
            mine = jnp.where(owner == t, stacked[g], 0.0).astype(BF16)
            total += lax.dot_general(
                mine, keys[t, :, g * HEAD_SIZE : (g + 1) * HEAD_SIZE],
                (((1,), (1,)), ((), ())), preferred_element_type=F32,
            )
        scores.append(total)
    probs = []
    for g in range(n_kv):
        s = jnp.where(alive, scores[g] / math.sqrt(HEAD_SIZE), -1e30)
        peak = jnp.max(s, axis=1, keepdims=True)
        e = jnp.where(alive, jnp.exp(s - peak), 0.0)
        probs.append((e / jnp.sum(e, axis=1, keepdims=True)).astype(BF16).astype(F32))
    for copy in value_copies:
        copy.wait()
    squares = jnp.zeros((rows, HEAD_SIZE), F32)
    for g in range(n_kv):
        total = jnp.zeros((block, HEAD_SIZE), F32)
        for t in range(rows):
            mine = jnp.where(owner == t, probs[g], 0.0).astype(BF16)
            total += jnp.dot(
                mine, values[t, :, g * HEAD_SIZE : (g + 1) * HEAD_SIZE],
                preferred_element_type=F32,
            )
        for j in range(per):
            at = slice((g * per + j) * HEAD_SIZE, (g * per + j + 1) * HEAD_SIZE)
            piece = tokens[:, at].astype(F32) + total[j * rows : (j + 1) * rows]
            resid_ref[:, at] = piece
            squares += piece * piece
    mean = jnp.sum(squares, axis=1, keepdims=True) / width
    scale = lax.rsqrt(mean + 1e-05)
    row_ref[:, :width] = (resid_ref[...] * scale * gain[...]).astype(BF16)
    row_at = lax.broadcasted_iota(jnp.int32, (rows, LANES), 0)
    lane = lax.broadcasted_iota(jnp.int32, (rows, LANES), 1)
    high = jnp.zeros((rows, LANES), F32)
    low = jnp.zeros((rows, LANES), F32)
    for t in range(rows):
        for k in range(routes.shape[0]):
            hit = row_at == t
            high += jnp.where(hit & (lane == routes[k, t]), weights[k, t], 0.0)
            low += jnp.where(hit & (lane == routes[k, t] + LANES // 2), weights[k, t], 0.0)
    low = low - low.astype(BF16).astype(F32)
    row_ref[:, width:] = (high.astype(BF16).astype(F32) + low).astype(BF16)


def attend(tokens, queries, keys, values, lengths, gain, routes, weights):
    rows, width = tokens.shape
    smem = pl.BlockSpec(memory_space=pltpu.SMEM)
    vmem = pl.BlockSpec(memory_space=pltpu.VMEM)
    hbm = pl.BlockSpec(memory_space=pl.ANY)
    return pl.pallas_call(
        attend_kernel,
        in_specs=[smem, smem, smem, vmem, vmem, vmem, hbm, hbm],
        out_specs=[vmem, vmem],
        out_shape=[
            jax.ShapeDtypeStruct((rows, width), F32),
            jax.ShapeDtypeStruct((rows, width + LANES), BF16),
        ],
        scratch_shapes=[
            pltpu.VMEM(keys.shape, BF16),
            pltpu.VMEM(values.shape, BF16),
            pltpu.SemaphoreType.DMA((rows,)),
            pltpu.SemaphoreType.DMA((rows,)),
        ],
        name="attend",
    )(lengths, routes.T, weights.T, tokens, queries, gain.reshape(1, width), keys, values)


def expert_kernel(n_pieces, chunk, wide, expert, *refs):
    pieces = refs[:n_pieces]
    gate_up_hbm, down_hbm = refs[n_pieces : n_pieces + 2]
    outs = refs[n_pieces + 2 : 2 * n_pieces + 2]
    x, gate_up, down, hidden, gate_sems, down_sems = refs[2 * n_pieces + 2 :]
    hidden_units, width = down_hbm.shape
    n_chunks = hidden_units // chunk
    n_wide = width // wide
    gate_copies = [
        pltpu.make_async_copy(
            gate_up_hbm.at[:, c * chunk : (c + 1) * chunk],
            gate_up.at[:, c * chunk : (c + 1) * chunk],
            gate_sems.at[c],
        )
        for c in range(n_chunks)
    ]
    down_copies = [
        pltpu.make_async_copy(
            down_hbm.at[c * chunk : (c + 1) * chunk],
            down.at[c * chunk : (c + 1) * chunk],
            down_sems.at[c],
        )
        for c in range(n_chunks)
    ]
    for copy in gate_copies + down_copies:
        copy.start()
    size = pieces[0].shape[0]
    factors = []
    for i in range(n_pieces):
        x[i * size : (i + 1) * size] = pieces[i][:, :width]
        meta = pieces[i][:, width:].astype(F32)
        lane = lax.broadcasted_iota(jnp.int32, meta.shape, 1)
        mine = lane % (LANES // 2) == expert[0]
        factors.append(jnp.sum(jnp.where(mine, meta, 0.0), axis=1, keepdims=True))
    for c in range(n_chunks):
        gate_copies[c].wait()
        at = slice(c * chunk, (c + 1) * chunk)
        both = [
            lax.dot_general(
                gate_up[i, at], x[...], (((1,), (1,)), ((), ())), preferred_element_type=F32
            )
            for i in range(2)
        ]
        hidden[at] = both[0] / (1.0 + jnp.exp(-both[0])) * both[1]
    turned = jnp.transpose(hidden[...]).astype(BF16)
    for copy in down_copies:
        copy.wait()
    for c in range(n_wide):
        at = slice(c * wide, (c + 1) * wide)
        total = jnp.dot(turned, down[:, at], preferred_element_type=F32)
        for i in range(n_pieces):
            part = total[i * size : (i + 1) * size] * factors[i]
            outs[i][:, at] = part.astype(BF16)


def experts(pieces, gate_up, down, expert):
    n_pieces = len(pieces)
    size, width = pieces[0].shape[0], pieces[0].shape[1] - LANES
    hidden_units = down.shape[0]
    chunk = next((c for c in (192, 96, 64, 32, 16) if hidden_units % c == 0), hidden_units)
    vmem = pl.BlockSpec(memory_space=pltpu.VMEM)
    hbm = pl.BlockSpec(memory_space=pl.ANY)
    return pl.pallas_call(
        functools.partial(expert_kernel, n_pieces, chunk, 768),
        in_specs=[pl.BlockSpec(memory_space=pltpu.SMEM)] + [vmem] * n_pieces + [hbm, hbm],
        out_specs=[vmem] * n_pieces,
        out_shape=[jax.ShapeDtypeStruct((size, width), BF16)] * n_pieces,
        scratch_shapes=[
            pltpu.VMEM((n_pieces * size, width), BF16),
            pltpu.VMEM(gate_up.shape, BF16),
            pltpu.VMEM(down.shape, BF16),
            pltpu.VMEM((hidden_units, n_pieces * size), F32),
            pltpu.SemaphoreType.DMA((hidden_units // chunk,)),
            pltpu.SemaphoreType.DMA((hidden_units // chunk,)),
        ],
        compiler_params=pltpu.CompilerParams(vmem_limit_bytes=60 * 2**20),
        name="experts",
    )(expert, *pieces, gate_up, down)


def swap(value, axis, bits):
    n = lax.axis_size(axis)
    return lax.ppermute(value, axis, [(i, i ^ bits) for i in range(n)])


def strides(size):
    steps, stride = [], 1
    while stride < size:
        radix = 4 if size // stride >= 4 else 2
        steps.append((stride, radix))
        stride *= radix
    return steps


def added(*parts):
    total = parts[0].astype(F32)
    for part in parts[1:]:
        total = total + part.astype(F32)
    return total.astype(BF16)


def shards(
    tokens, queries, stored_keys, stored_values, lengths, norm_gain, routes, route_weights,
    gate_up, down_proj,
):
    n_side = lax.axis_size("side")
    rows = tokens.shape[0]
    resid, row = attend(
        tokens, queries, stored_keys, stored_values, lengths, norm_gain, routes, route_weights
    )
    tp_steps = strides(lax.axis_size("tp"))
    held = row
    for stride, radix in tp_steps:
        held = jnp.concatenate(
            [held] + [swap(held, "tp", stride * k) for k in range(1, radix)], axis=0
        )
    pieces = [held]
    side_bits = []
    bit = n_side // 2
    while bit:
        side_bits.append(bit)
        pieces = pieces + [swap(piece, "side", bit) for piece in pieces]
        bit //= 2
    expert = lax.axis_index("side").astype(jnp.int32).reshape(1)
    parts = list(experts(pieces, gate_up[0], down_proj[0], expert))
    for bit in reversed(side_bits):
        half = len(parts) // 2
        parts = [
            added(parts[i], swap(parts[half + i], "side", bit)) for i in range(half)
        ]
    total = parts[0]
    for stride, radix in reversed(tp_steps):
        size = total.shape[0] // radix
        own = total[:size]
        other = [
            swap(total[k * size : (k + 1) * size], "tp", stride * k) for k in range(1, radix)
        ]
        if size == rows:
            mixed = resid + own.astype(F32)
            for part in other:
                mixed = mixed + part.astype(F32)
            return mixed.astype(BF16)
        total = added(own, *other)


def solution(mesh):
    rows = ("groups", "side", "tp")
    placed = (
        P(rows, None),
        P(rows, None),
        P(rows, None, None),
        P(rows, None, None),
        P(rows),
        P(),
        P(rows, None),
        P(rows, None),
        P("side", None, "tp", None),
        P("side", "tp", None),
    )
    return jax.shard_map(
        shards, mesh=mesh, in_specs=placed, out_specs=P(rows, None), check_vma=False
    )
```

```python
import functools
import math

import jax
import jax.numpy as jnp
from jax import lax
from jax.experimental import pallas as pl
from jax.experimental.pallas import tpu as pltpu
from jax.sharding import PartitionSpec as P

HEAD_SIZE = 128
LANES = 128
F32 = jnp.float32
BF16 = jnp.bfloat16


def attend_kernel(
    lengths, routes, weights, tokens, queries, gain, keys_hbm, values_hbm, ahead_hbm,
    resid_ref, row_ref, ahead, keys, values, key_sems, value_sems, ahead_sems,
):
    rows, positions, kv_width = keys_hbm.shape
    width = tokens.shape[1]
    n_kv = kv_width // HEAD_SIZE
    per = width // kv_width
    key_copies = [
        pltpu.make_async_copy(keys_hbm.at[t], keys.at[t], key_sems.at[t]) for t in range(rows)
    ]
    value_copies = [
        pltpu.make_async_copy(values_hbm.at[t], values.at[t], value_sems.at[t])
        for t in range(rows)
    ]
    ahead_copies = ahead_parts(ahead_hbm, ahead, ahead_sems, 0)
    for copy in key_copies + value_copies + ahead_copies:
        copy.start()
    block = per * rows
    owner = lax.broadcasted_iota(jnp.int32, (block, 1), 0) % rows
    length = jnp.zeros((block, 1), jnp.int32)
    for t in range(rows):
        length = jnp.where(owner == t, lengths[t], length)
    alive = lax.broadcasted_iota(jnp.int32, (block, positions), 1) < length
    q = queries[...].astype(F32)
    stacked = []
    for g in range(n_kv):
        heads = [
            q[:, (g * per + j) * HEAD_SIZE : (g * per + j + 1) * HEAD_SIZE] for j in range(per)
        ]
        stacked.append(jnp.concatenate(heads, axis=0))
    for copy in key_copies:
        copy.wait()
    scores = []
    for g in range(n_kv):
        total = jnp.zeros((block, positions), F32)
        for t in range(rows):
            mine = jnp.where(owner == t, stacked[g], 0.0).astype(BF16)
            total += lax.dot_general(
                mine, keys[t, :, g * HEAD_SIZE : (g + 1) * HEAD_SIZE],
                (((1,), (1,)), ((), ())), preferred_element_type=F32,
            )
        scores.append(total)
    probs = []
    for g in range(n_kv):
        s = jnp.where(alive, scores[g] / math.sqrt(HEAD_SIZE), -1e30)
        peak = jnp.max(s, axis=1, keepdims=True)
        e = jnp.where(alive, jnp.exp(s - peak), 0.0)
        probs.append((e / jnp.sum(e, axis=1, keepdims=True)).astype(BF16).astype(F32))
    for copy in value_copies:
        copy.wait()
    squares = jnp.zeros((rows, HEAD_SIZE), F32)
    for g in range(n_kv):
        total = jnp.zeros((block, HEAD_SIZE), F32)
        for t in range(rows):
            mine = jnp.where(owner == t, probs[g], 0.0).astype(BF16)
            total += jnp.dot(
                mine, values[t, :, g * HEAD_SIZE : (g + 1) * HEAD_SIZE],
                preferred_element_type=F32,
            )
        for j in range(per):
            at = slice((g * per + j) * HEAD_SIZE, (g * per + j + 1) * HEAD_SIZE)
            piece = tokens[:, at].astype(F32) + total[j * rows : (j + 1) * rows]
            resid_ref[:, at] = piece
            squares += piece * piece
    mean = jnp.sum(squares, axis=1, keepdims=True) / width
    scale = lax.rsqrt(mean + 1e-05)
    row_ref[:, :width] = (resid_ref[...] * scale * gain[...]).astype(BF16)
    row_at = lax.broadcasted_iota(jnp.int32, (rows, LANES), 0)
    lane = lax.broadcasted_iota(jnp.int32, (rows, LANES), 1)
    high = jnp.zeros((rows, LANES), F32)
    low = jnp.zeros((rows, LANES), F32)
    for t in range(rows):
        for k in range(routes.shape[0]):
            hit = row_at == t
            high += jnp.where(hit & (lane == routes[k, t]), weights[k, t], 0.0)
            low += jnp.where(hit & (lane == routes[k, t] + LANES // 2), weights[k, t], 0.0)
    low = low - low.astype(BF16).astype(F32)
    row_ref[:, width:] = (high.astype(BF16).astype(F32) + low).astype(BF16)
    for copy in ahead_copies:
        copy.wait()


def thirds(hidden_units):
    return 3 if hidden_units % 48 == 0 else 1


def ahead_parts(source, target, sems, part):
    size = target.shape[1]
    return [
        pltpu.make_async_copy(
            source.at[i, part * size : (part + 1) * size], target.at[i], sems.at[i]
        )
        for i in range(2)
    ]


def ahead_shape(gate_up):
    two, hidden_units, width = gate_up.shape
    return pltpu.VMEM((two, hidden_units // thirds(hidden_units), width), gate_up.dtype)


def ahead_kernel(part, source, target, sems):
    copies = ahead_parts(source, target, sems, part)
    for copy in copies:
        copy.start()
    for copy in copies:
        copy.wait()


def bring(gate_up, part):
    shape = ahead_shape(gate_up)
    return pl.pallas_call(
        functools.partial(ahead_kernel, part),
        in_specs=[pl.BlockSpec(memory_space=pltpu.HBM)],
        out_specs=pl.BlockSpec(memory_space=pltpu.VMEM),
        out_shape=shape,
        scratch_shapes=[pltpu.SemaphoreType.DMA((2,))],
        cost_estimate=pl.CostEstimate(
            flops=0, transcendentals=0, bytes_accessed=2 * math.prod(shape.shape)
        ),
        compiler_params=pltpu.CompilerParams(vmem_limit_bytes=2**20),
        name="bring",
    )(in_hbm(gate_up))


def attend(tokens, queries, keys, values, lengths, gain, routes, weights, gate_up):
    rows, width = tokens.shape
    smem = pl.BlockSpec(memory_space=pltpu.SMEM)
    vmem = pl.BlockSpec(memory_space=pltpu.VMEM)
    hbm = pl.BlockSpec(memory_space=pltpu.HBM)
    return pl.pallas_call(
        attend_kernel,
        in_specs=[smem, smem, smem, vmem, vmem, vmem, hbm, hbm, hbm],
        out_specs=[vmem, vmem, vmem],
        out_shape=[
            pltpu.VMEM((rows, width), F32),
            pltpu.VMEM((rows, width + LANES), BF16),
            ahead_shape(gate_up),
        ],
        scratch_shapes=[
            pltpu.VMEM(keys.shape, BF16),
            pltpu.VMEM(values.shape, BF16),
            pltpu.SemaphoreType.DMA((rows,)),
            pltpu.SemaphoreType.DMA((rows,)),
            pltpu.SemaphoreType.DMA((2,)),
        ],
        compiler_params=pltpu.CompilerParams(vmem_limit_bytes=12 * 2**20),
        name="attend",
    )(
        lengths, routes.T, weights.T, tokens, queries, gain.reshape(1, width),
        in_hbm(keys), in_hbm(values), in_hbm(gate_up),
    )


def expert_kernel(n_pieces, n_parts, chunk, wide, *refs):
    expert = lax.axis_index("side").astype(jnp.int32)
    pieces = refs[:n_pieces]
    parts = refs[n_pieces : n_pieces + n_parts]
    down_hbm = refs[n_pieces + n_parts]
    outs = refs[n_pieces + n_parts + 1 : 2 * n_pieces + n_parts + 1]
    x, down, hidden, down_sems = refs[2 * n_pieces + n_parts + 1 :]
    hidden_units, width = down_hbm.shape
    part_units = hidden_units // n_parts
    down_copies = [
        pltpu.make_async_copy(
            down_hbm.at[c * part_units : (c + 1) * part_units],
            down.at[c * part_units : (c + 1) * part_units],
            down_sems.at[c],
        )
        for c in range(n_parts)
    ]
    for copy in down_copies:
        copy.start()
    size = pieces[0].shape[0]
    factors = []
    for i in range(n_pieces):
        x[i * size : (i + 1) * size] = pieces[i][:, :width]
        meta = pieces[i][:, width:].astype(F32)
        lane = lax.broadcasted_iota(jnp.int32, meta.shape, 1)
        mine = lane % (LANES // 2) == expert
        factors.append(jnp.sum(jnp.where(mine, meta, 0.0), axis=1, keepdims=True))
    for p in range(n_parts):
        for c in range(part_units // chunk):
            both = [
                lax.dot_general(
                    parts[p][i, c * chunk : (c + 1) * chunk], x[...],
                    (((1,), (1,)), ((), ())), preferred_element_type=F32,
                )
                for i in range(2)
            ]
            first = p * part_units + c * chunk
            hidden[first : first + chunk] = both[0] / (1.0 + jnp.exp(-both[0])) * both[1]
    turned = jnp.transpose(hidden[...]).astype(BF16)
    for copy in down_copies:
        copy.wait()
    for c in range(width // wide):
        at = slice(c * wide, (c + 1) * wide)
        total = jnp.dot(turned, down[:, at], preferred_element_type=F32)
        for i in range(n_pieces):
            part = total[i * size : (i + 1) * size] * factors[i]
            outs[i][:, at] = part.astype(BF16)


def in_vmem(value):
    return pltpu.with_memory_space_constraint(value, pltpu.VMEM)


def in_hbm(value):
    return pltpu.with_memory_space_constraint(value, pltpu.HBM)


def join_kernel(*refs):
    out = refs[-1]
    out[...] = jnp.concatenate([ref[...].astype(F32) for ref in refs[:-1]], axis=0).astype(BF16)


def join(pieces):
    size, width = pieces[0].shape
    vmem = pl.BlockSpec(memory_space=pltpu.VMEM)
    return pl.pallas_call(
        join_kernel,
        in_specs=[vmem] * len(pieces),
        out_specs=vmem,
        out_shape=pltpu.VMEM((len(pieces) * size, width), BF16),
        compiler_params=pltpu.CompilerParams(vmem_limit_bytes=2 * 2**20),
        name="join",
    )(*map(in_vmem, pieces))


def experts(pieces, parts, down):
    n_pieces, n_parts = len(pieces), len(parts)
    size, width = pieces[0].shape[0], pieces[0].shape[1] - LANES
    hidden_units = down.shape[0]
    part_units = hidden_units // n_parts
    chunk = part_units // 2 if part_units % 32 == 0 else part_units
    vmem = pl.BlockSpec(memory_space=pltpu.VMEM)
    return pl.pallas_call(
        functools.partial(expert_kernel, n_pieces, n_parts, chunk, 768),
        in_specs=[vmem] * (n_pieces + n_parts)
        + [pl.BlockSpec(memory_space=pltpu.HBM)],
        out_specs=[vmem] * n_pieces,
        out_shape=[pltpu.VMEM((size, width), BF16)] * n_pieces,
        scratch_shapes=[
            pltpu.VMEM((n_pieces * size, width), BF16),
            pltpu.VMEM(down.shape, BF16),
            pltpu.VMEM((hidden_units, n_pieces * size), F32),
            pltpu.SemaphoreType.DMA((n_parts,)),
        ],
        compiler_params=pltpu.CompilerParams(vmem_limit_bytes=19 * 2**20),
        name="experts",
    )(*map(in_vmem, pieces), *map(in_vmem, parts), in_hbm(down))


def swap(value, axis, bits):
    n = lax.axis_size(axis)
    return lax.ppermute(value, axis, [(i, i ^ bits) for i in range(n)])


def strides(size):
    steps, stride = [], 1
    while stride < size:
        radix = 4 if size // stride >= 4 else 2
        steps.append((stride, radix))
        stride *= radix
    return steps


def added(*parts):
    total = parts[0].astype(F32)
    for part in parts[1:]:
        total = total + part.astype(F32)
    return total.astype(BF16)


def shards(
    tokens, queries, stored_keys, stored_values, lengths, norm_gain, routes, route_weights,
    gate_up, down_proj,
):
    n_side = lax.axis_size("side")
    rows = tokens.shape[0]
    resid, row, first_part = attend(
        tokens, queries, stored_keys, stored_values, lengths, norm_gain, routes, route_weights,
        gate_up[0],
    )
    weight_parts = [first_part]
    waiting = list(range(1, thirds(gate_up.shape[2])))

    def beside(values):
        if not waiting:
            return values
        brought = bring(gate_up[0], waiting.pop(0))
        brought, *values = lax.optimization_barrier((brought, *values))
        weight_parts.append(brought)
        return values

    tp_steps = strides(lax.axis_size("tp"))
    held = row
    for stride, radix in tp_steps:
        others = beside([swap(held, "tp", stride * k) for k in range(1, radix)])
        held = join([held] + others)
    pieces = [held]
    side_bits = []
    bit = n_side // 2
    while bit:
        side_bits.append(bit)
        pieces = pieces + beside([swap(piece, "side", bit) for piece in pieces])
        bit //= 2
    while waiting:
        weight_parts.append(bring(gate_up[0], waiting.pop(0)))
    parts = list(experts(pieces, weight_parts, down_proj[0]))
    for bit in reversed(side_bits):
        half = len(parts) // 2
        parts = [
            added(parts[i], swap(parts[half + i], "side", bit)) for i in range(half)
        ]
    total = parts[0]
    for stride, radix in reversed(tp_steps):
        size = total.shape[0] // radix
        own = total[:size]
        other = [
            swap(total[k * size : (k + 1) * size], "tp", stride * k) for k in range(1, radix)
        ]
        if size == rows:
            mixed = resid + own.astype(F32)
            for part in other:
                mixed = mixed + part.astype(F32)
            return mixed.astype(BF16)
        total = added(own, *other)


def solution(mesh):
    rows = ("groups", "side", "tp")
    placed = (
        P(rows, None),
        P(rows, None),
        P(rows, None, None),
        P(rows, None, None),
        P(rows),
        P(),
        P(rows, None),
        P(rows, None),
        P("side", None, "tp", None),
        P("side", "tp", None),
    )
    return jax.shard_map(
        shards, mesh=mesh, in_specs=placed, out_specs=P(rows, None), check_vma=False
    )
```

```python
import functools
import math

import jax
import jax.numpy as jnp
from jax import lax
from jax.experimental import pallas as pl
from jax.experimental.pallas import tpu as pltpu
from jax.sharding import PartitionSpec as P

HEAD_SIZE = 128
LANES = 128
F32 = jnp.float32
BF16 = jnp.bfloat16


def attend_kernel(
    *refs,
):
    small_hbm, (keys_hbm, values_hbm, ahead_hbm) = refs[:6], refs[6:9]
    resid_ref, row_ref, ahead = refs[9:12]
    small, (keys, values) = refs[12:18], refs[18:20]
    small_sems, key_sems, value_sems, ahead_sems = refs[20:]
    queries, tokens, gain, lengths, routes, weights = small
    rows, positions, kv_width = keys_hbm.shape
    width = tokens.shape[1]
    small_copies = [
        pltpu.make_async_copy(source, target, small_sems.at[i])
        for i, (source, target) in enumerate(zip(small_hbm, small))
    ]
    for copy in small_copies:
        copy.start()
    n_kv = kv_width // HEAD_SIZE
    per = width // kv_width
    key_copies = [
        pltpu.make_async_copy(keys_hbm.at[t], keys.at[t], key_sems.at[t]) for t in range(rows)
    ]
    value_copies = [
        pltpu.make_async_copy(values_hbm.at[t], values.at[t], value_sems.at[t])
        for t in range(rows)
    ]
    ahead_copies = ahead_parts(ahead_hbm, ahead, ahead_sems, 0)
    for copy in key_copies + value_copies + ahead_copies:
        copy.start()
    for copy in small_copies:
        copy.wait()
    block = per * rows
    owner = lax.broadcasted_iota(jnp.int32, (block, 1), 0) % rows
    length = jnp.zeros((block, 1), jnp.int32)
    for t in range(rows):
        length = jnp.where(owner == t, lengths[0, t], length)
    alive = lax.broadcasted_iota(jnp.int32, (block, positions), 1) < length
    q = queries[...].astype(F32)
    stacked = []
    for g in range(n_kv):
        heads = [
            q[:, (g * per + j) * HEAD_SIZE : (g * per + j + 1) * HEAD_SIZE] for j in range(per)
        ]
        stacked.append(jnp.concatenate(heads, axis=0))
    for copy in key_copies:
        copy.wait()
    scores = []
    for g in range(n_kv):
        total = jnp.zeros((block, positions), F32)
        for t in range(rows):
            mine = jnp.where(owner == t, stacked[g], 0.0).astype(BF16)
            total += lax.dot_general(
                mine, keys[t, :, g * HEAD_SIZE : (g + 1) * HEAD_SIZE],
                (((1,), (1,)), ((), ())), preferred_element_type=F32,
            )
        scores.append(total)
    probs = []
    for g in range(n_kv):
        s = jnp.where(alive, scores[g] / math.sqrt(HEAD_SIZE), -1e30)
        peak = jnp.max(s, axis=1, keepdims=True)
        e = jnp.where(alive, jnp.exp(s - peak), 0.0)
        probs.append((e / jnp.sum(e, axis=1, keepdims=True)).astype(BF16).astype(F32))
    for copy in value_copies:
        copy.wait()
    squares = jnp.zeros((rows, HEAD_SIZE), F32)
    for g in range(n_kv):
        total = jnp.zeros((block, HEAD_SIZE), F32)
        for t in range(rows):
            mine = jnp.where(owner == t, probs[g], 0.0).astype(BF16)
            total += jnp.dot(
                mine, values[t, :, g * HEAD_SIZE : (g + 1) * HEAD_SIZE],
                preferred_element_type=F32,
            )
        for j in range(per):
            at = slice((g * per + j) * HEAD_SIZE, (g * per + j + 1) * HEAD_SIZE)
            piece = tokens[:, at].astype(F32) + total[j * rows : (j + 1) * rows]
            resid_ref[:, at] = piece
            squares += piece * piece
    mean = jnp.sum(squares, axis=1, keepdims=True) / width
    scale = lax.rsqrt(mean + 1e-05)
    row_ref[:, :width] = (resid_ref[...] * scale * gain[...]).astype(BF16)
    row_at = lax.broadcasted_iota(jnp.int32, (rows, LANES), 0)
    lane = lax.broadcasted_iota(jnp.int32, (rows, LANES), 1)
    high = jnp.zeros((rows, LANES), F32)
    low = jnp.zeros((rows, LANES), F32)
    for t in range(rows):
        for k in range(routes.shape[0]):
            hit = row_at == t
            high += jnp.where(hit & (lane == routes[k, t]), weights[k, t], 0.0)
            low += jnp.where(hit & (lane == routes[k, t] + LANES // 2), weights[k, t], 0.0)
    low = low - low.astype(BF16).astype(F32)
    row_ref[:, width:] = (high.astype(BF16).astype(F32) + low).astype(BF16)
    for copy in ahead_copies:
        copy.wait()


def spans(hidden_units):
    sizes = [hidden_units]
    if hidden_units > 1024 and hidden_units % 16 == 0:
        sizes = [512, 256, hidden_units - 768]
    return [(sum(sizes[:i]), size) for i, size in enumerate(sizes)]


def ahead_parts(source, target, sems, first):
    size = target.shape[1]
    return [
        pltpu.make_async_copy(source.at[i, first : first + size], target.at[i], sems.at[i])
        for i in range(2)
    ]


def ahead_shape(gate_up, part):
    two, hidden_units, width = gate_up.shape
    return pltpu.VMEM((two, spans(hidden_units)[part][1], width), gate_up.dtype)


def ahead_kernel(first, source, target, sems):
    copies = ahead_parts(source, target, sems, first)
    for copy in copies:
        copy.start()
    for copy in copies:
        copy.wait()


def bring(gate_up, part):
    shape = ahead_shape(gate_up, part)
    return pl.pallas_call(
        functools.partial(ahead_kernel, spans(gate_up.shape[1])[part][0]),
        in_specs=[pl.BlockSpec(memory_space=pltpu.HBM)],
        out_specs=pl.BlockSpec(memory_space=pltpu.VMEM),
        out_shape=shape,
        scratch_shapes=[pltpu.SemaphoreType.DMA((2,))],
        cost_estimate=pl.CostEstimate(
            flops=0, transcendentals=0, bytes_accessed=2 * math.prod(shape.shape)
        ),
        compiler_params=pltpu.CompilerParams(vmem_limit_bytes=2**20),
        name="bring",
    )(in_hbm(gate_up))


def attend(tokens, queries, keys, values, lengths, gain, routes, weights, gate_up):
    rows, width = tokens.shape
    vmem = pl.BlockSpec(memory_space=pltpu.VMEM)
    operands = [
        queries, tokens, gain.reshape(1, width), lengths.reshape(1, rows), routes.T, weights.T,
        keys, values, gate_up,
    ]
    return pl.pallas_call(
        attend_kernel,
        in_specs=[pl.BlockSpec(memory_space=pltpu.HBM)] * len(operands),
        out_specs=[vmem, vmem, vmem],
        out_shape=[
            pltpu.VMEM((rows, width), F32),
            pltpu.VMEM((rows, width + LANES), BF16),
            ahead_shape(gate_up, 0),
        ],
        scratch_shapes=[
            pltpu.VMEM(queries.shape, BF16),
            pltpu.VMEM(tokens.shape, BF16),
            pltpu.VMEM((1, width), F32),
            pltpu.SMEM((1, rows), jnp.int32),
            pltpu.SMEM((routes.shape[1], rows), jnp.int32),
            pltpu.SMEM((routes.shape[1], rows), F32),
            pltpu.VMEM(keys.shape, BF16),
            pltpu.VMEM(values.shape, BF16),
            pltpu.SemaphoreType.DMA((6,)),
            pltpu.SemaphoreType.DMA((rows,)),
            pltpu.SemaphoreType.DMA((rows,)),
            pltpu.SemaphoreType.DMA((2,)),
        ],
        compiler_params=pltpu.CompilerParams(vmem_limit_bytes=12 * 2**20),
        name="attend",
    )(*map(in_hbm, operands))


def weighted_down(turned, down, factors, outs):
    wide = 768
    size = outs[0].shape[0]
    for c in range(down.shape[1] // wide):
        at = slice(c * wide, (c + 1) * wide)
        total = jnp.dot(turned, down[:, at], preferred_element_type=F32)
        for i, out in enumerate(outs):
            out[:, at] = (total[i * size : (i + 1) * size] * factors[i]).astype(BF16)


def expert_kernel(n_pieces, n_parts, *refs):
    expert = lax.axis_index("side").astype(jnp.int32)
    pieces = refs[:n_pieces]
    parts = refs[n_pieces : n_pieces + n_parts]
    down_hbm = refs[n_pieces + n_parts]
    outs = refs[n_pieces + n_parts + 1 : 2 * n_pieces + n_parts + 1]
    turned_ref, factor_ref, later = refs[2 * n_pieces + n_parts + 1 : 2 * n_pieces + n_parts + 4]
    x, down, down_sems = refs[2 * n_pieces + n_parts + 4 :]
    width = x.shape[1]
    half = width // 2
    down_copies = [
        pltpu.make_async_copy(down_hbm.at[:, :half], down, down_sems.at[0]),
        pltpu.make_async_copy(down_hbm.at[:, half:], later, down_sems.at[1]),
    ]
    for copy in down_copies:
        copy.start()
    size = pieces[0].shape[0]
    factors = []
    for i in range(n_pieces):
        at = slice(i * size, (i + 1) * size)
        x[at] = pieces[i][:, :width]
        meta = pieces[i][:, width:].astype(F32)
        lane = lax.broadcasted_iota(jnp.int32, meta.shape, 1)
        mine = lane % (LANES // 2) == expert
        factors.append(jnp.sum(jnp.where(mine, meta, 0.0), axis=1, keepdims=True))
        factor_ref[at] = jnp.broadcast_to(factors[i], (size, LANES))
    first = 0
    for part in parts:
        units = part.shape[1]
        gate, up = [
            lax.dot_general(
                x[...], part[i], (((1,), (1,)), ((), ())), preferred_element_type=F32
            )
            for i in range(2)
        ]
        turned_ref[:, first : first + units] = (gate / (1.0 + jnp.exp(-gate)) * up).astype(BF16)
        first += units
    down_copies[0].wait()
    weighted_down(turned_ref[...], down, factors, outs)
    down_copies[1].wait()


def later_kernel(n_pieces, turned, factor_ref, down, *outs):
    size = outs[0].shape[0]
    factors = [factor_ref[i * size : (i + 1) * size, :1] for i in range(n_pieces)]
    weighted_down(turned[...], down, factors, outs)


def join_kernel(*refs):
    out = refs[-1]
    out[...] = jnp.concatenate([ref[...].astype(F32) for ref in refs[:-1]], axis=0).astype(BF16)


def join(pieces):
    size, width = pieces[0].shape
    vmem = pl.BlockSpec(memory_space=pltpu.VMEM)
    return pl.pallas_call(
        join_kernel,
        in_specs=[vmem] * len(pieces),
        out_specs=vmem,
        out_shape=pltpu.VMEM((len(pieces) * size, width), BF16),
        compiler_params=pltpu.CompilerParams(vmem_limit_bytes=2 * 2**20),
        name="join",
    )(*map(in_vmem, pieces))


def experts(pieces, parts, down):
    n_pieces, n_parts = len(pieces), len(parts)
    size, width = pieces[0].shape[0], pieces[0].shape[1] - LANES
    hidden_units, half = down.shape[0], width // 2
    rows = n_pieces * size
    vmem = pl.BlockSpec(memory_space=pltpu.VMEM)
    out_shape = [pltpu.VMEM((size, half), BF16)] * n_pieces
    *first, turned, factor, later = pl.pallas_call(
        functools.partial(expert_kernel, n_pieces, n_parts),
        in_specs=[vmem] * (n_pieces + n_parts) + [pl.BlockSpec(memory_space=pltpu.HBM)],
        out_specs=[vmem] * (n_pieces + 3),
        out_shape=out_shape
        + [
            pltpu.VMEM((rows, hidden_units), BF16),
            pltpu.VMEM((rows, LANES), F32),
            pltpu.VMEM((hidden_units, half), BF16),
        ],
        scratch_shapes=[
            pltpu.VMEM((rows, width), BF16),
            pltpu.VMEM((hidden_units, half), BF16),
            pltpu.SemaphoreType.DMA((2,)),
        ],
        compiler_params=pltpu.CompilerParams(vmem_limit_bytes=16 * 2**20),
        name="experts",
    )(*map(in_vmem, pieces), *map(in_vmem, parts), in_hbm(down))
    second = pl.pallas_call(
        functools.partial(later_kernel, n_pieces),
        in_specs=[vmem] * 3,
        out_specs=[vmem] * n_pieces,
        out_shape=out_shape,
        cost_estimate=pl.CostEstimate(
            flops=2 * rows * hidden_units * half, transcendentals=0,
            bytes_accessed=2 * hidden_units * half,
        ),
        compiler_params=pltpu.CompilerParams(vmem_limit_bytes=4 * 2**20),
        name="later",
    )(in_vmem(turned), in_vmem(factor), in_vmem(later))
    return list(first), list(second)


def in_vmem(value):
    return pltpu.with_memory_space_constraint(value, pltpu.VMEM)


def in_hbm(value):
    return pltpu.with_memory_space_constraint(value, pltpu.HBM)


def swap(value, axis, bits):
    n = lax.axis_size(axis)
    return lax.ppermute(value, axis, [(i, i ^ bits) for i in range(n)])


def strides(size):
    steps, stride = [], 1
    while stride < size:
        radix = 4 if size // stride >= 4 else 2
        steps.append((stride, radix))
        stride *= radix
    return steps


def split(parts):
    half = len(parts) // 2
    return parts[:half], parts[half:]


def added(*parts):
    total = parts[0].astype(F32)
    for part in parts[1:]:
        total = total + part.astype(F32)
    return total.astype(BF16)


def shards(
    tokens, queries, stored_keys, stored_values, lengths, norm_gain, routes, route_weights,
    gate_up, down_proj,
):
    n_side = lax.axis_size("side")
    resid, row, first_part = attend(
        tokens, queries, stored_keys, stored_values, lengths, norm_gain, routes, route_weights,
        gate_up[0],
    )
    weight_parts = [first_part]
    waiting = list(range(1, len(spans(gate_up.shape[2]))))

    def beside(values):
        if not waiting:
            return values
        brought = bring(gate_up[0], waiting.pop(0))
        brought, *values = lax.optimization_barrier((brought, *values))
        weight_parts.append(brought)
        return values

    tp_steps = strides(lax.axis_size("tp"))
    held = row
    for stride, radix in tp_steps:
        others = beside([swap(held, "tp", stride * k) for k in range(1, radix)])
        held = join([held] + others)
    pieces = [held]
    side_bits = []
    bit = n_side // 2
    while bit:
        side_bits.append(bit)
        pieces = pieces + beside([swap(piece, "side", bit) for piece in pieces])
        bit //= 2
    while waiting:
        weight_parts.append(bring(gate_up[0], waiting.pop(0)))
    halves = experts(pieces, weight_parts, down_proj[0])
    for bit in reversed(side_bits):
        halves = [
            [added(near, swap(far, "side", bit)) for near, far in zip(*split(parts))]
            for parts in halves
        ]
    totals = [parts[0] for parts in halves]
    for stride, radix in reversed(tp_steps):
        size = totals[0].shape[0] // radix
        gathered = []
        for total in totals:
            others = [
                swap(total[k * size : (k + 1) * size], "tp", stride * k) for k in range(1, radix)
            ]
            gathered.append([total[:size]] + others)
        totals = [added(*parts) for parts in gathered]
    mixed = []
    half = resid.shape[1] // 2
    for i, parts in enumerate(gathered):
        total = resid[:, i * half : (i + 1) * half]
        for part in parts:
            total = total + part.astype(F32)
        mixed.append(total.astype(BF16))
    return jnp.concatenate(mixed, axis=1)


def solution(mesh):
    rows = ("groups", "side", "tp")
    placed = (
        P(rows, None),
        P(rows, None),
        P(rows, None, None),
        P(rows, None, None),
        P(rows),
        P(),
        P(rows, None),
        P(rows, None),
        P("side", None, "tp", None),
        P("side", "tp", None),
    )
    return jax.shard_map(
        shards, mesh=mesh, in_specs=placed, out_specs=P(rows, None), check_vma=False
    )
```

```python
import functools
import math

import jax
import jax.numpy as jnp
from jax import lax
from jax.experimental import pallas as pl
from jax.experimental.pallas import tpu as pltpu
from jax.sharding import PartitionSpec as P

HEAD_SIZE = 128
LANES = 128
F32 = jnp.float32
BF16 = jnp.bfloat16


def attend_kernel(
    *refs,
):
    small_hbm, (keys_hbm, values_hbm, ahead_hbm) = refs[:6], refs[6:9]
    resid_ref, row_ref, ahead = refs[9:12]
    small, (keys, values) = refs[12:18], refs[18:20]
    small_sems, key_sems, value_sems, ahead_sems = refs[20:]
    queries, tokens, gain, lengths, routes, weights = small
    rows, positions, kv_width = keys_hbm.shape
    width = tokens.shape[1]
    small_copies = [
        pltpu.make_async_copy(source, target, small_sems.at[i])
        for i, (source, target) in enumerate(zip(small_hbm, small))
    ]
    for copy in small_copies:
        copy.start()
    n_kv = kv_width // HEAD_SIZE
    per = width // kv_width
    key_copies = [
        pltpu.make_async_copy(keys_hbm.at[t], keys.at[t], key_sems.at[t]) for t in range(rows)
    ]
    value_copies = [
        pltpu.make_async_copy(values_hbm.at[t], values.at[t], value_sems.at[t])
        for t in range(rows)
    ]
    ahead_copies = ahead_parts(ahead_hbm, ahead, ahead_sems, 0)
    for copy in key_copies + value_copies + ahead_copies:
        copy.start()
    for copy in small_copies:
        copy.wait()
    block = per * rows
    owner = lax.broadcasted_iota(jnp.int32, (block, 1), 0) % rows
    length = jnp.zeros((block, 1), jnp.int32)
    for t in range(rows):
        length = jnp.where(owner == t, lengths[0, t], length)
    alive = lax.broadcasted_iota(jnp.int32, (block, positions), 1) < length
    q = queries[...].astype(F32)
    stacked = []
    for g in range(n_kv):
        heads = [
            q[:, (g * per + j) * HEAD_SIZE : (g * per + j + 1) * HEAD_SIZE] for j in range(per)
        ]
        stacked.append(jnp.concatenate(heads, axis=0))
    for copy in key_copies:
        copy.wait()
    scores = []
    for g in range(n_kv):
        total = jnp.zeros((block, positions), F32)
        for t in range(rows):
            mine = jnp.where(owner == t, stacked[g], 0.0).astype(BF16)
            total += lax.dot_general(
                mine, keys[t, :, g * HEAD_SIZE : (g + 1) * HEAD_SIZE],
                (((1,), (1,)), ((), ())), preferred_element_type=F32,
            )
        scores.append(total)
    probs = []
    for g in range(n_kv):
        s = jnp.where(alive, scores[g] / math.sqrt(HEAD_SIZE), -1e30)
        peak = jnp.max(s, axis=1, keepdims=True)
        e = jnp.where(alive, jnp.exp(s - peak), 0.0)
        probs.append((e / jnp.sum(e, axis=1, keepdims=True)).astype(BF16).astype(F32))
    for copy in value_copies:
        copy.wait()
    squares = jnp.zeros((rows, HEAD_SIZE), F32)
    for g in range(n_kv):
        total = jnp.zeros((block, HEAD_SIZE), F32)
        for t in range(rows):
            mine = jnp.where(owner == t, probs[g], 0.0).astype(BF16)
            total += jnp.dot(
                mine, values[t, :, g * HEAD_SIZE : (g + 1) * HEAD_SIZE],
                preferred_element_type=F32,
            )
        for j in range(per):
            at = slice((g * per + j) * HEAD_SIZE, (g * per + j + 1) * HEAD_SIZE)
            piece = tokens[:, at].astype(F32) + total[j * rows : (j + 1) * rows]
            resid_ref[:, at] = piece
            squares += piece * piece
    mean = jnp.sum(squares, axis=1, keepdims=True) / width
    scale = lax.rsqrt(mean + 1e-05)
    row_ref[:, :width] = (resid_ref[...] * scale * gain[...]).astype(BF16)
    row_at = lax.broadcasted_iota(jnp.int32, (rows, LANES), 0)
    lane = lax.broadcasted_iota(jnp.int32, (rows, LANES), 1)
    high = jnp.zeros((rows, LANES), F32)
    low = jnp.zeros((rows, LANES), F32)
    for t in range(rows):
        for k in range(routes.shape[0]):
            hit = row_at == t
            high += jnp.where(hit & (lane == routes[k, t]), weights[k, t], 0.0)
            low += jnp.where(hit & (lane == routes[k, t] + LANES // 2), weights[k, t], 0.0)
    low = low - low.astype(BF16).astype(F32)
    row_ref[:, width:] = (high.astype(BF16).astype(F32) + low).astype(BF16)
    for copy in ahead_copies:
        copy.wait()


def spans(hidden_units):
    sizes = [hidden_units]
    if hidden_units > 1024 and hidden_units % 16 == 0:
        sizes = [256, 256, 256, hidden_units - 768]
    return [(sum(sizes[:i]), size) for i, size in enumerate(sizes)]


def ahead_parts(source, target, sems, first):
    size = target.shape[1]
    return [
        pltpu.make_async_copy(source.at[i, first : first + size], target.at[i], sems.at[i])
        for i in range(2)
    ]


def ahead_shape(gate_up, part):
    two, hidden_units, width = gate_up.shape
    return pltpu.VMEM((two, spans(hidden_units)[part][1], width), gate_up.dtype)


def ahead_kernel(first, source, target, sems):
    copies = ahead_parts(source, target, sems, first)
    for copy in copies:
        copy.start()
    for copy in copies:
        copy.wait()


def bring(gate_up, part):
    shape = ahead_shape(gate_up, part)
    return pl.pallas_call(
        functools.partial(ahead_kernel, spans(gate_up.shape[1])[part][0]),
        in_specs=[pl.BlockSpec(memory_space=pltpu.HBM)],
        out_specs=pl.BlockSpec(memory_space=pltpu.VMEM),
        out_shape=shape,
        scratch_shapes=[pltpu.SemaphoreType.DMA((2,))],
        cost_estimate=pl.CostEstimate(
            flops=0, transcendentals=0, bytes_accessed=2 * math.prod(shape.shape)
        ),
        compiler_params=pltpu.CompilerParams(vmem_limit_bytes=2**20),
        name="bring",
    )(in_hbm(gate_up))


def attend(tokens, queries, keys, values, lengths, gain, routes, weights, gate_up):
    rows, width = tokens.shape
    vmem = pl.BlockSpec(memory_space=pltpu.VMEM)
    operands = [
        queries, tokens, gain.reshape(1, width), lengths.reshape(1, rows), routes.T, weights.T,
        keys, values, gate_up,
    ]
    return pl.pallas_call(
        attend_kernel,
        in_specs=[pl.BlockSpec(memory_space=pltpu.HBM)] * len(operands),
        out_specs=[vmem, vmem, vmem],
        out_shape=[
            pltpu.VMEM((rows, width), F32),
            pltpu.VMEM((rows, width + LANES), BF16),
            ahead_shape(gate_up, 0),
        ],
        scratch_shapes=[
            pltpu.VMEM(queries.shape, BF16),
            pltpu.VMEM(tokens.shape, BF16),
            pltpu.VMEM((1, width), F32),
            pltpu.SMEM((1, rows), jnp.int32),
            pltpu.SMEM((routes.shape[1], rows), jnp.int32),
            pltpu.SMEM((routes.shape[1], rows), F32),
            pltpu.VMEM(keys.shape, BF16),
            pltpu.VMEM(values.shape, BF16),
            pltpu.SemaphoreType.DMA((6,)),
            pltpu.SemaphoreType.DMA((rows,)),
            pltpu.SemaphoreType.DMA((rows,)),
            pltpu.SemaphoreType.DMA((2,)),
        ],
        compiler_params=pltpu.CompilerParams(vmem_limit_bytes=12 * 2**20),
        name="attend",
    )(*map(in_hbm, operands))


def weighted_down(turned, down, factors, outs):
    wide = 768
    size = outs[0].shape[0]
    for c in range(down.shape[1] // wide):
        at = slice(c * wide, (c + 1) * wide)
        total = jnp.dot(turned, down[:, at], preferred_element_type=F32)
        for i, out in enumerate(outs):
            out[:, at] = (total[i * size : (i + 1) * size] * factors[i]).astype(BF16)


def expert_kernel(n_pieces, n_parts, *refs):
    expert = lax.axis_index("side").astype(jnp.int32)
    pieces = refs[:n_pieces]
    parts = refs[n_pieces : n_pieces + n_parts]
    down_hbm = refs[n_pieces + n_parts]
    outs = refs[n_pieces + n_parts + 1 : 2 * n_pieces + n_parts + 1]
    turned_ref, factor_ref, later = refs[2 * n_pieces + n_parts + 1 : 2 * n_pieces + n_parts + 4]
    x, down, down_sems = refs[2 * n_pieces + n_parts + 4 :]
    width = x.shape[1]
    half = width // 2
    quarter = half // 2
    down_copies = [
        pltpu.make_async_copy(
            down_hbm.at[:, c * quarter : (c + 1) * quarter],
            (down, later)[c // 2].at[:, c % 2 * quarter : (c % 2 + 1) * quarter],
            down_sems.at[c],
        )
        for c in range(4)
    ]
    to_start = list(down_copies)
    to_start.pop(0).start()
    size = pieces[0].shape[0]
    factors = []
    for i in range(n_pieces):
        at = slice(i * size, (i + 1) * size)
        x[at] = pieces[i][:, :width]
        meta = pieces[i][:, width:].astype(F32)
        lane = lax.broadcasted_iota(jnp.int32, meta.shape, 1)
        mine = lane % (LANES // 2) == expert
        factors.append(jnp.sum(jnp.where(mine, meta, 0.0), axis=1, keepdims=True))
        factor_ref[at] = jnp.broadcast_to(factors[i], (size, LANES))
    first = 0
    for part in parts:
        units = part.shape[1]
        if to_start and part is not parts[-1]:
            to_start.pop(0).start()
        gate, up = [
            lax.dot_general(
                x[...], part[i], (((1,), (1,)), ((), ())), preferred_element_type=F32
            )
            for i in range(2)
        ]
        turned_ref[:, first : first + units] = (gate / (1.0 + jnp.exp(-gate)) * up).astype(BF16)
        first += units
    for copy in to_start:
        copy.start()
    for copy in down_copies[:2]:
        copy.wait()
    weighted_down(turned_ref[...], down, factors, outs)
    for copy in down_copies[2:]:
        copy.wait()


def later_kernel(n_pieces, turned, factor_ref, down, *outs):
    size = outs[0].shape[0]
    factors = [factor_ref[i * size : (i + 1) * size, :1] for i in range(n_pieces)]
    weighted_down(turned[...], down, factors, outs)


def join_kernel(*refs):
    out = refs[-1]
    out[...] = jnp.concatenate([ref[...].astype(F32) for ref in refs[:-1]], axis=0).astype(BF16)


def join(pieces):
    size, width = pieces[0].shape
    vmem = pl.BlockSpec(memory_space=pltpu.VMEM)
    return pl.pallas_call(
        join_kernel,
        in_specs=[vmem] * len(pieces),
        out_specs=vmem,
        out_shape=pltpu.VMEM((len(pieces) * size, width), BF16),
        compiler_params=pltpu.CompilerParams(vmem_limit_bytes=2 * 2**20),
        name="join",
    )(*map(in_vmem, pieces))


def experts(pieces, parts, down):
    n_pieces, n_parts = len(pieces), len(parts)
    size, width = pieces[0].shape[0], pieces[0].shape[1] - LANES
    hidden_units, half = down.shape[0], width // 2
    rows = n_pieces * size
    vmem = pl.BlockSpec(memory_space=pltpu.VMEM)
    out_shape = [pltpu.VMEM((size, half), BF16)] * n_pieces
    *first, turned, factor, later = pl.pallas_call(
        functools.partial(expert_kernel, n_pieces, n_parts),
        in_specs=[vmem] * (n_pieces + n_parts) + [pl.BlockSpec(memory_space=pltpu.HBM)],
        out_specs=[vmem] * (n_pieces + 3),
        out_shape=out_shape
        + [
            pltpu.VMEM((rows, hidden_units), BF16),
            pltpu.VMEM((rows, LANES), F32),
            pltpu.VMEM((hidden_units, half), BF16),
        ],
        scratch_shapes=[
            pltpu.VMEM((rows, width), BF16),
            pltpu.VMEM((hidden_units, half), BF16),
            pltpu.SemaphoreType.DMA((4,)),
        ],
        compiler_params=pltpu.CompilerParams(vmem_limit_bytes=16 * 2**20),
        name="experts",
    )(*map(in_vmem, pieces), *map(in_vmem, parts), in_hbm(down))
    second = pl.pallas_call(
        functools.partial(later_kernel, n_pieces),
        in_specs=[vmem] * 3,
        out_specs=[vmem] * n_pieces,
        out_shape=out_shape,
        cost_estimate=pl.CostEstimate(
            flops=2 * rows * hidden_units * half, transcendentals=0,
            bytes_accessed=2 * hidden_units * half,
        ),
        compiler_params=pltpu.CompilerParams(vmem_limit_bytes=4 * 2**20),
        name="later",
    )(in_vmem(turned), in_vmem(factor), in_vmem(later))
    return list(first), list(second)


def in_vmem(value):
    return pltpu.with_memory_space_constraint(value, pltpu.VMEM)


def in_hbm(value):
    return pltpu.with_memory_space_constraint(value, pltpu.HBM)


def swap(value, axis, bits):
    n = lax.axis_size(axis)
    return lax.ppermute(value, axis, [(i, i ^ bits) for i in range(n)])


def strides(size):
    return [size >> i for i in range(1, size.bit_length())]


def added(*parts):
    total = parts[0].astype(F32)
    for part in parts[1:]:
        total = total + part.astype(F32)
    return total.astype(BF16)


def exchanged(parts, axis, stride):
    half = len(parts) // 2
    return [added(parts[i], swap(parts[half + i], axis, stride)) for i in range(half)]


def shards(
    tokens, queries, stored_keys, stored_values, lengths, norm_gain, routes, route_weights,
    gate_up, down_proj,
):
    resid, row, first_part = attend(
        tokens, queries, stored_keys, stored_values, lengths, norm_gain, routes, route_weights,
        gate_up[0],
    )
    weight_parts = [first_part]
    waiting = list(range(1, len(spans(gate_up.shape[2]))))

    def beside(values):
        if not waiting:
            return values
        brought = bring(gate_up[0], waiting.pop(0))
        brought, *values = lax.optimization_barrier((brought, *values))
        weight_parts.append(brought)
        return values

    tp_steps = strides(lax.axis_size("tp"))
    side_steps = strides(lax.axis_size("side"))
    held = row
    for stride in tp_steps:
        held = join([held] + beside([swap(held, "tp", stride)]))
    pieces = [held]
    for stride in side_steps:
        pieces = pieces + beside([swap(piece, "side", stride) for piece in pieces])
    while waiting:
        weight_parts.append(bring(gate_up[0], waiting.pop(0)))
    halves = experts(pieces, weight_parts, down_proj[0])
    parts = [
        jnp.concatenate(both, axis=1)
        for both in zip(*[exchanged(half, "side", side_steps[-1]) for half in halves])
    ]
    for stride in reversed(side_steps[:-1]):
        parts = exchanged(parts, "side", stride)
    total = parts[0]
    for stride in reversed(tp_steps[1:]):
        half = total.shape[0] // 2
        total = added(total[:half], swap(total[half:], "tp", stride))
    rows = resid.shape[0]
    last = swap(total[rows:], "tp", tp_steps[0])
    return (resid + total[:rows].astype(F32) + last.astype(F32)).astype(BF16)


def solution(mesh):
    rows = ("groups", "side", "tp")
    placed = (
        P(rows, None),
        P(rows, None),
        P(rows, None, None),
        P(rows, None, None),
        P(rows),
        P(),
        P(rows, None),
        P(rows, None),
        P("side", None, "tp", None),
        P("side", "tp", None),
    )
    return jax.shard_map(
        shards, mesh=mesh, in_specs=placed, out_specs=P(rows, None), check_vma=False
    )
```

```python
import functools
import math

import jax
import jax.numpy as jnp
from jax import lax
from jax.experimental import pallas as pl
from jax.experimental.pallas import tpu as pltpu
from jax.sharding import PartitionSpec as P

HEAD_SIZE = 128
LANES = 128
F32 = jnp.float32
BF16 = jnp.bfloat16


def attend_kernel(
    *refs,
):
    small_hbm, (keys_hbm, values_hbm, ahead_hbm) = refs[:6], refs[6:9]
    resid_ref, row_ref, ahead = refs[9:12]
    small, (keys, values) = refs[12:18], refs[18:20]
    small_sems, key_sems, value_sems, ahead_sems = refs[20:]
    queries, tokens, gain, lengths, routes, weights = small
    rows, positions, kv_width = keys_hbm.shape
    width = tokens.shape[1]
    small_copies = [
        pltpu.make_async_copy(source, target, small_sems.at[i])
        for i, (source, target) in enumerate(zip(small_hbm, small))
    ]
    for copy in small_copies:
        copy.start()
    n_kv = kv_width // HEAD_SIZE
    per = width // kv_width
    key_copies = [
        pltpu.make_async_copy(keys_hbm.at[t], keys.at[t], key_sems.at[t]) for t in range(rows)
    ]
    value_copies = [
        pltpu.make_async_copy(values_hbm.at[t], values.at[t], value_sems.at[t])
        for t in range(rows)
    ]
    ahead_copies = ahead_parts(ahead_hbm, ahead, ahead_sems, 0)
    for copy in key_copies + value_copies + ahead_copies:
        copy.start()
    for copy in small_copies:
        copy.wait()
    block = per * rows
    owner = lax.broadcasted_iota(jnp.int32, (block, 1), 0) % rows
    length = jnp.zeros((block, 1), jnp.int32)
    for t in range(rows):
        length = jnp.where(owner == t, lengths[0, t], length)
    alive = lax.broadcasted_iota(jnp.int32, (block, positions), 1) < length
    q = queries[...].astype(F32)
    stacked = []
    for g in range(n_kv):
        heads = [
            q[:, (g * per + j) * HEAD_SIZE : (g * per + j + 1) * HEAD_SIZE] for j in range(per)
        ]
        stacked.append(jnp.concatenate(heads, axis=0))
    for copy in key_copies:
        copy.wait()
    scores = []
    for g in range(n_kv):
        total = jnp.zeros((block, positions), F32)
        for t in range(rows):
            mine = jnp.where(owner == t, stacked[g], 0.0).astype(BF16)
            total += lax.dot_general(
                mine, keys[t, :, g * HEAD_SIZE : (g + 1) * HEAD_SIZE],
                (((1,), (1,)), ((), ())), preferred_element_type=F32,
            )
        scores.append(total)
    probs = []
    for g in range(n_kv):
        s = jnp.where(alive, scores[g] / math.sqrt(HEAD_SIZE), -1e30)
        peak = jnp.max(s, axis=1, keepdims=True)
        e = jnp.where(alive, jnp.exp(s - peak), 0.0)
        probs.append((e / jnp.sum(e, axis=1, keepdims=True)).astype(BF16).astype(F32))
    for copy in value_copies:
        copy.wait()
    squares = jnp.zeros((rows, HEAD_SIZE), F32)
    for g in range(n_kv):
        total = jnp.zeros((block, HEAD_SIZE), F32)
        for t in range(rows):
            mine = jnp.where(owner == t, probs[g], 0.0).astype(BF16)
            total += jnp.dot(
                mine, values[t, :, g * HEAD_SIZE : (g + 1) * HEAD_SIZE],
                preferred_element_type=F32,
            )
        for j in range(per):
            at = slice((g * per + j) * HEAD_SIZE, (g * per + j + 1) * HEAD_SIZE)
            piece = tokens[:, at].astype(F32) + total[j * rows : (j + 1) * rows]
            resid_ref[:, at] = piece
            squares += piece * piece
    mean = jnp.sum(squares, axis=1, keepdims=True) / width
    scale = lax.rsqrt(mean + 1e-05)
    row_ref[:, :width] = (resid_ref[...] * scale * gain[...]).astype(BF16)
    row_at = lax.broadcasted_iota(jnp.int32, (rows, LANES), 0)
    lane = lax.broadcasted_iota(jnp.int32, (rows, LANES), 1)
    high = jnp.zeros((rows, LANES), F32)
    low = jnp.zeros((rows, LANES), F32)
    for t in range(rows):
        for k in range(routes.shape[0]):
            hit = row_at == t
            high += jnp.where(hit & (lane == routes[k, t]), weights[k, t], 0.0)
            low += jnp.where(hit & (lane == routes[k, t] + LANES // 2), weights[k, t], 0.0)
    low = low - low.astype(BF16).astype(F32)
    row_ref[:, width:] = (high.astype(BF16).astype(F32) + low).astype(BF16)
    for copy in ahead_copies:
        copy.wait()


def spans(hidden_units):
    sizes = [hidden_units]
    if hidden_units > 1024 and hidden_units % 16 == 0:
        sizes = [256, 256, 256, hidden_units - 768]
    return [(sum(sizes[:i]), size) for i, size in enumerate(sizes)]


def ahead_parts(source, target, sems, first):
    size = target.shape[1]
    return [
        pltpu.make_async_copy(source.at[i, first : first + size], target.at[i], sems.at[i])
        for i in range(2)
    ]


def ahead_shape(gate_up, part):
    two, hidden_units, width = gate_up.shape
    return pltpu.VMEM((two, spans(hidden_units)[part][1], width), gate_up.dtype)


def bring_kernel(cuts, *refs):
    n = len(cuts)
    sources, targets, sems = refs[:n], refs[n : 2 * n], refs[2 * n]
    copies = [
        pltpu.make_async_copy(sources[i].at[cut], targets[i], sems.at[i])
        for i, cut in enumerate(cuts)
    ]
    for copy in copies:
        copy.start()
    for copy in copies:
        copy.wait()


def bring(arrays, cuts, shapes):
    n = len(arrays)
    return pl.pallas_call(
        functools.partial(bring_kernel, cuts),
        in_specs=[pl.BlockSpec(memory_space=pltpu.HBM)] * n,
        out_specs=[pl.BlockSpec(memory_space=pltpu.VMEM)] * n,
        out_shape=[pltpu.VMEM(shape, BF16) for shape in shapes],
        scratch_shapes=[pltpu.SemaphoreType.DMA((n,))],
        cost_estimate=pl.CostEstimate(
            flops=0, transcendentals=0, bytes_accessed=2 * sum(map(math.prod, shapes))
        ),
        compiler_params=pltpu.CompilerParams(vmem_limit_bytes=2**20),
        name="bring",
    )(*map(in_hbm, arrays))


def attend(tokens, queries, keys, values, lengths, gain, routes, weights, gate_up):
    rows, width = tokens.shape
    vmem = pl.BlockSpec(memory_space=pltpu.VMEM)
    operands = [
        queries, tokens, gain.reshape(1, width), lengths.reshape(1, rows), routes.T, weights.T,
        keys, values, gate_up,
    ]
    return pl.pallas_call(
        attend_kernel,
        in_specs=[pl.BlockSpec(memory_space=pltpu.HBM)] * len(operands),
        out_specs=[vmem, vmem, vmem],
        out_shape=[
            pltpu.VMEM((rows, width), F32),
            pltpu.VMEM((rows, width + LANES), BF16),
            ahead_shape(gate_up, 0),
        ],
        scratch_shapes=[
            pltpu.VMEM(queries.shape, BF16),
            pltpu.VMEM(tokens.shape, BF16),
            pltpu.VMEM((1, width), F32),
            pltpu.SMEM((1, rows), jnp.int32),
            pltpu.SMEM((routes.shape[1], rows), jnp.int32),
            pltpu.SMEM((routes.shape[1], rows), F32),
            pltpu.VMEM(keys.shape, BF16),
            pltpu.VMEM(values.shape, BF16),
            pltpu.SemaphoreType.DMA((6,)),
            pltpu.SemaphoreType.DMA((rows,)),
            pltpu.SemaphoreType.DMA((rows,)),
            pltpu.SemaphoreType.DMA((2,)),
        ],
        compiler_params=pltpu.CompilerParams(vmem_limit_bytes=12 * 2**20),
        name="attend",
    )(*map(in_hbm, operands))


def expert_kernel(n_pieces, n_parts, n_ready, *refs):
    expert = lax.axis_index("side").astype(jnp.int32)
    refs = list(refs)

    def take(n):
        taken, refs[:n] = refs[:n], []
        return taken

    pieces, parts, ready, (down_hbm,) = take(n_pieces), take(n_parts), take(n_ready), take(1)
    outs, loaded, (x, hidden, down_sems) = take(n_pieces), take(4 - n_ready), take(3)
    width = x.shape[1]
    quarters = ready + loaded
    columns = width // 4
    down_copies = [
        pltpu.make_async_copy(
            down_hbm.at[:, c * columns : (c + 1) * columns], quarters[c], down_sems.at[c]
        )
        for c in range(n_ready, 4)
    ]
    to_start = list(down_copies)
    to_start.pop(0).start()
    size = pieces[0].shape[0]
    factors = []
    for i in range(n_pieces):
        at = slice(i * size, (i + 1) * size)
        x[at] = pieces[i][:, :width]
        meta = pieces[i][:, width:].astype(F32)
        lane = lax.broadcasted_iota(jnp.int32, meta.shape, 1)
        mine = lane % (LANES // 2) == expert
        factors.append(jnp.sum(jnp.where(mine, meta, 0.0), axis=1, keepdims=True))
    first = 0
    for part in parts:
        units = part.shape[1]
        if part is parts[-1]:
            to_start.pop(0).start()
        gate, up = [
            lax.dot_general(
                x[...], part[i], (((1,), (1,)), ((), ())), preferred_element_type=F32
            )
            for i in range(2)
        ]
        hidden[:, first : first + units] = (gate / (1.0 + jnp.exp(-gate)) * up).astype(BF16)
        first += units
    for q, quarter in enumerate(quarters):
        if q >= n_ready:
            down_copies[q - n_ready].wait()
            if to_start:
                to_start.pop(0).start()
        wide = columns // 2
        for c in range(2):
            total = jnp.dot(
                hidden[...], quarter[:, c * wide : (c + 1) * wide], preferred_element_type=F32
            )
            at = slice(q * columns + c * wide, q * columns + (c + 1) * wide)
            for i, out in enumerate(outs):
                part = total[i * size : (i + 1) * size] * factors[i]
                out[:, at] = part.astype(BF16)


def join_kernel(*refs):
    out = refs[-1]
    out[...] = jnp.concatenate([ref[...].astype(F32) for ref in refs[:-1]], axis=0).astype(BF16)


def join(pieces):
    size, width = pieces[0].shape
    vmem = pl.BlockSpec(memory_space=pltpu.VMEM)
    return pl.pallas_call(
        join_kernel,
        in_specs=[vmem] * len(pieces),
        out_specs=vmem,
        out_shape=pltpu.VMEM((len(pieces) * size, width), BF16),
        compiler_params=pltpu.CompilerParams(vmem_limit_bytes=2 * 2**20),
        name="join",
    )(*map(in_vmem, pieces))


def experts(pieces, parts, ready, down):
    n_pieces, n_parts, n_ready = len(pieces), len(parts), len(ready)
    size, width = pieces[0].shape[0], pieces[0].shape[1] - LANES
    hidden_units = down.shape[0]
    rows = n_pieces * size
    vmem = pl.BlockSpec(memory_space=pltpu.VMEM)
    return pl.pallas_call(
        functools.partial(expert_kernel, n_pieces, n_parts, n_ready),
        in_specs=[vmem] * (n_pieces + n_parts + n_ready) + [pl.BlockSpec(memory_space=pltpu.HBM)],
        out_specs=[vmem] * n_pieces,
        out_shape=[pltpu.VMEM((size, width), BF16)] * n_pieces,
        scratch_shapes=[pltpu.VMEM((hidden_units, width // 4), BF16)] * (4 - n_ready)
        + [
            pltpu.VMEM((rows, width), BF16),
            pltpu.VMEM((rows, hidden_units), BF16),
            pltpu.SemaphoreType.DMA((4,)),
        ],
        compiler_params=pltpu.CompilerParams(vmem_limit_bytes=20 * 2**20),
        name="experts",
    )(*map(in_vmem, [*pieces, *parts, *ready]), in_hbm(down))


def in_vmem(value):
    return pltpu.with_memory_space_constraint(value, pltpu.VMEM)


def in_hbm(value):
    return pltpu.with_memory_space_constraint(value, pltpu.HBM)


def swap(value, axis, bits):
    n = lax.axis_size(axis)
    return lax.ppermute(value, axis, [(i, i ^ bits) for i in range(n)])


def strides(size):
    return [size >> i for i in range(1, size.bit_length())]


def added(*parts):
    total = parts[0].astype(F32)
    for part in parts[1:]:
        total = total + part.astype(F32)
    return total.astype(BF16)


def exchanged(parts, axis, stride):
    half = len(parts) // 2
    return [added(parts[i], swap(parts[half + i], axis, stride)) for i in range(half)]


def shards(
    tokens, queries, stored_keys, stored_values, lengths, norm_gain, routes, route_weights,
    gate_up, down_proj,
):
    resid, row, first_part = attend(
        tokens, queries, stored_keys, stored_values, lengths, norm_gain, routes, route_weights,
        gate_up[0],
    )
    gate_up, down = gate_up[0], down_proj[0]
    two, hidden_units, width = gate_up.shape
    weight_parts, ready = [first_part], []
    waiting = [
        ((slice(None), slice(first, first + size)), (two, size, width))
        for first, size in spans(hidden_units)[1:]
    ]

    def beside(values, down_quarter=False):
        if not waiting:
            return values
        cut, shape = waiting.pop(0)
        arrays, cuts, shapes = [gate_up], [cut], [shape]
        if down_quarter:
            arrays.append(down)
            cuts.append((slice(None), slice(0, width // 4)))
            shapes.append((hidden_units, width // 4))
        brought = bring(arrays, cuts, shapes)
        *brought, values = lax.optimization_barrier((*brought, values))
        weight_parts.append(brought[0])
        ready.extend(brought[1:])
        return values

    tp_steps = strides(lax.axis_size("tp"))
    side_steps = strides(lax.axis_size("side"))
    held = row
    for i, stride in enumerate(tp_steps):
        held = join([held, beside(swap(held, "tp", stride), i == 1)])
    pieces = [held]
    for stride in side_steps:
        pieces = pieces + beside([swap(piece, "side", stride) for piece in pieces])
    while waiting:
        beside(())
    parts = experts(pieces, weight_parts, ready, down)
    for stride in reversed(side_steps):
        half = len(parts) // 2
        parts = [added(parts[i], swap(parts[half + i], "side", stride)) for i in range(half)]
    total = parts[0].astype(F32)
    while tp_steps:
        near, tp_steps = tp_steps[-2:], tp_steps[:-2]
        away = [0]
        for stride in near:
            away = away + [stride ^ k for k in away]
        size = total.shape[0] // len(away)
        sent = total.astype(BF16)
        total = total[:size]
        if not tp_steps:
            total = resid + total
        far_first = sorted(range(1, len(away)), key=lambda i: -away[i])
        for i in far_first:
            total = total + swap(sent[i * size : (i + 1) * size], "tp", away[i]).astype(F32)
    return total.astype(BF16)


def solution(mesh):
    rows = ("groups", "side", "tp")
    placed = (
        P(rows, None),
        P(rows, None),
        P(rows, None, None),
        P(rows, None, None),
        P(rows),
        P(),
        P(rows, None),
        P(rows, None),
        P("side", None, "tp", None),
        P("side", "tp", None),
    )
    return jax.shard_map(
        shards, mesh=mesh, in_specs=placed, out_specs=P(rows, None), check_vma=False
    )
```

```python
import functools
import math

import jax
import jax.numpy as jnp
from jax import lax
from jax.experimental import pallas as pl
from jax.experimental.pallas import tpu as pltpu
from jax.sharding import PartitionSpec as P

HEAD_SIZE = 128
LANES = 128
EARLY_BLOCKS = (3, 1)
BLOCKS = 8
F32 = jnp.float32
BF16 = jnp.bfloat16


def attend_kernel(
    *refs,
):
    small_hbm, (keys_hbm, values_hbm, ahead_hbm) = refs[:6], refs[6:9]
    resid_ref, row_ref, ahead = refs[9:12]
    small, (keys, values) = refs[12:18], refs[18:20]
    small_sems, key_sems, value_sems, ahead_sems = refs[20:]
    queries, tokens, gain, lengths, routes, weights = small
    rows, positions, kv_width = keys_hbm.shape
    width = tokens.shape[1]
    small_copies = [
        pltpu.make_async_copy(source, target, small_sems.at[i])
        for i, (source, target) in enumerate(zip(small_hbm, small))
    ]
    for copy in small_copies:
        copy.start()
    n_kv = kv_width // HEAD_SIZE
    per = width // kv_width
    key_copies = [
        pltpu.make_async_copy(keys_hbm.at[t], keys.at[t], key_sems.at[t]) for t in range(rows)
    ]
    value_copies = [
        pltpu.make_async_copy(values_hbm.at[t], values.at[t], value_sems.at[t])
        for t in range(rows)
    ]
    ahead_copies = ahead_parts(ahead_hbm, ahead, ahead_sems, 0)
    for copy in key_copies + value_copies + ahead_copies:
        copy.start()
    for copy in small_copies:
        copy.wait()
    block = per * rows
    owner = lax.broadcasted_iota(jnp.int32, (block, 1), 0) % rows
    length = jnp.zeros((block, 1), jnp.int32)
    for t in range(rows):
        length = jnp.where(owner == t, lengths[0, t], length)
    alive = lax.broadcasted_iota(jnp.int32, (block, positions), 1) < length
    q = queries[...].astype(F32)
    stacked = []
    for g in range(n_kv):
        heads = [
            q[:, (g * per + j) * HEAD_SIZE : (g * per + j + 1) * HEAD_SIZE] for j in range(per)
        ]
        stacked.append(jnp.concatenate(heads, axis=0))
    for copy in key_copies:
        copy.wait()
    scores = []
    for g in range(n_kv):
        total = jnp.zeros((block, positions), F32)
        for t in range(rows):
            mine = jnp.where(owner == t, stacked[g], 0.0).astype(BF16)
            total += lax.dot_general(
                mine, keys[t, :, g * HEAD_SIZE : (g + 1) * HEAD_SIZE],
                (((1,), (1,)), ((), ())), preferred_element_type=F32,
            )
        scores.append(total)
    probs = []
    for g in range(n_kv):
        s = jnp.where(alive, scores[g] / math.sqrt(HEAD_SIZE), -1e30)
        peak = jnp.max(s, axis=1, keepdims=True)
        e = jnp.where(alive, jnp.exp(s - peak), 0.0)
        probs.append((e / jnp.sum(e, axis=1, keepdims=True)).astype(BF16).astype(F32))
    for copy in value_copies:
        copy.wait()
    squares = jnp.zeros((rows, HEAD_SIZE), F32)
    for g in range(n_kv):
        total = jnp.zeros((block, HEAD_SIZE), F32)
        for t in range(rows):
            mine = jnp.where(owner == t, probs[g], 0.0).astype(BF16)
            total += jnp.dot(
                mine, values[t, :, g * HEAD_SIZE : (g + 1) * HEAD_SIZE],
                preferred_element_type=F32,
            )
        for j in range(per):
            at = slice((g * per + j) * HEAD_SIZE, (g * per + j + 1) * HEAD_SIZE)
            piece = tokens[:, at].astype(F32) + total[j * rows : (j + 1) * rows]
            resid_ref[:, at] = piece
            squares += piece * piece
    mean = jnp.sum(squares, axis=1, keepdims=True) / width
    scale = lax.rsqrt(mean + 1e-05)
    row_ref[:, :width] = (resid_ref[...] * scale * gain[...]).astype(BF16)
    row_at = lax.broadcasted_iota(jnp.int32, (rows, LANES), 0)
    lane = lax.broadcasted_iota(jnp.int32, (rows, LANES), 1)
    high = jnp.zeros((rows, LANES), F32)
    low = jnp.zeros((rows, LANES), F32)
    for t in range(rows):
        for k in range(routes.shape[0]):
            hit = row_at == t
            high += jnp.where(hit & (lane == routes[k, t]), weights[k, t], 0.0)
            low += jnp.where(hit & (lane == routes[k, t] + LANES // 2), weights[k, t], 0.0)
    low = low - low.astype(BF16).astype(F32)
    row_ref[:, width:] = (high.astype(BF16).astype(F32) + low).astype(BF16)
    for copy in ahead_copies:
        copy.wait()


def spans(hidden_units):
    n = 3 if hidden_units > 1024 and hidden_units % 48 == 0 else 1
    size = hidden_units // n
    return [(i * size, size) for i in range(n)]


def ahead_parts(source, target, sems, first):
    size = target.shape[1]
    return [
        pltpu.make_async_copy(source.at[i, first : first + size], target.at[i], sems.at[i])
        for i in range(2)
    ]


def ahead_shape(gate_up, part):
    two, hidden_units, width = gate_up.shape
    return pltpu.VMEM((two, spans(hidden_units)[part][1], width), gate_up.dtype)


def bring_kernel(cuts, *refs):
    n = len(cuts)
    sources, targets, sems = refs[:n], refs[n : 2 * n], refs[2 * n]
    copies = [
        pltpu.make_async_copy(sources[i].at[cut], targets[i], sems.at[i])
        for i, cut in enumerate(cuts)
    ]
    for copy in copies:
        copy.start()
    for copy in copies:
        copy.wait()


def bring(arrays, cuts, shapes):
    n = len(arrays)
    return pl.pallas_call(
        functools.partial(bring_kernel, cuts),
        in_specs=[pl.BlockSpec(memory_space=pltpu.HBM)] * n,
        out_specs=[pl.BlockSpec(memory_space=pltpu.VMEM)] * n,
        out_shape=[pltpu.VMEM(shape, BF16) for shape in shapes],
        scratch_shapes=[pltpu.SemaphoreType.DMA((n,))],
        cost_estimate=pl.CostEstimate(
            flops=0, transcendentals=0, bytes_accessed=2 * sum(map(math.prod, shapes))
        ),
        compiler_params=pltpu.CompilerParams(vmem_limit_bytes=2**20),
        name="bring",
    )(*map(in_hbm, arrays))


def attend(tokens, queries, keys, values, lengths, gain, routes, weights, gate_up):
    rows, width = tokens.shape
    vmem = pl.BlockSpec(memory_space=pltpu.VMEM)
    operands = [
        queries, tokens, gain.reshape(1, width), lengths.reshape(1, rows), routes.T, weights.T,
        keys, values, gate_up,
    ]
    return pl.pallas_call(
        attend_kernel,
        in_specs=[pl.BlockSpec(memory_space=pltpu.HBM)] * len(operands),
        out_specs=[vmem, vmem, vmem],
        out_shape=[
            pltpu.VMEM((rows, width), F32),
            pltpu.VMEM((rows, width + LANES), BF16),
            ahead_shape(gate_up, 0),
        ],
        scratch_shapes=[
            pltpu.VMEM(queries.shape, BF16),
            pltpu.VMEM(tokens.shape, BF16),
            pltpu.VMEM((1, width), F32),
            pltpu.SMEM((1, rows), jnp.int32),
            pltpu.SMEM((routes.shape[1], rows), jnp.int32),
            pltpu.SMEM((routes.shape[1], rows), F32),
            pltpu.VMEM(keys.shape, BF16),
            pltpu.VMEM(values.shape, BF16),
            pltpu.SemaphoreType.DMA((6,)),
            pltpu.SemaphoreType.DMA((rows,)),
            pltpu.SemaphoreType.DMA((rows,)),
            pltpu.SemaphoreType.DMA((2,)),
        ],
        compiler_params=pltpu.CompilerParams(vmem_limit_bytes=12 * 2**20),
        name="attend",
    )(*map(in_hbm, operands))


def expert_kernel(n_pieces, n_parts, n_ready, *refs):
    expert = lax.axis_index("side").astype(jnp.int32)
    refs = list(refs)

    def take(n):
        taken, refs[:n] = refs[:n], []
        return taken

    pieces, parts, ready, (down_hbm,) = take(n_pieces), take(n_parts), take(n_ready), take(1)
    outs, (loaded, x, hidden, down_sems) = take(n_pieces), take(4)
    width = x.shape[1]
    wide = width // BLOCKS
    skip, half = width - loaded.shape[1], loaded.shape[1] // 2
    down_copies = [
        pltpu.make_async_copy(
            down_hbm.at[:, skip + c * half : skip + (c + 1) * half],
            loaded.at[:, c * half : (c + 1) * half],
            down_sems.at[c],
        )
        for c in range(2)
    ]
    for copy in down_copies:
        copy.start()
    size = pieces[0].shape[0]
    factors = []
    for i in range(n_pieces):
        at = slice(i * size, (i + 1) * size)
        x[at] = pieces[i][:, :width]
        meta = pieces[i][:, width:].astype(F32)
        lane = lax.broadcasted_iota(jnp.int32, meta.shape, 1)
        mine = lane % (LANES // 2) == expert
        factors.append(jnp.sum(jnp.where(mine, meta, 0.0), axis=1, keepdims=True))
    first = 0
    for part in parts:
        units = part.shape[1]
        gate, up = [
            lax.dot_general(
                x[...], part[i], (((1,), (1,)), ((), ())), preferred_element_type=F32
            )
            for i in range(2)
        ]
        hidden[:, first : first + units] = (gate / (1.0 + jnp.exp(-gate)) * up).astype(BF16)
        first += units
    first = 0
    for down in ready + [loaded]:
        for c in range(down.shape[1] // wide):
            if down is loaded and c * wide % half == 0:
                down_copies[c * wide // half].wait()
            block = down[:, c * wide : (c + 1) * wide]
            total = jnp.dot(hidden[...], block, preferred_element_type=F32)
            for i, out in enumerate(outs):
                part = total[i * size : (i + 1) * size] * factors[i]
                out[:, first : first + wide] = part.astype(BF16)
            first += wide


def join_kernel(*refs):
    out = refs[-1]
    out[...] = jnp.concatenate([ref[...].astype(F32) for ref in refs[:-1]], axis=0).astype(BF16)


def join(pieces):
    size, width = pieces[0].shape
    vmem = pl.BlockSpec(memory_space=pltpu.VMEM)
    return pl.pallas_call(
        join_kernel,
        in_specs=[vmem] * len(pieces),
        out_specs=vmem,
        out_shape=pltpu.VMEM((len(pieces) * size, width), BF16),
        compiler_params=pltpu.CompilerParams(vmem_limit_bytes=2 * 2**20),
        name="join",
    )(*map(in_vmem, pieces))


def experts(pieces, parts, ready, down):
    n_pieces, n_parts, n_ready = len(pieces), len(parts), len(ready)
    size, width = pieces[0].shape[0], pieces[0].shape[1] - LANES
    hidden_units = down.shape[0]
    rows = n_pieces * size
    vmem = pl.BlockSpec(memory_space=pltpu.VMEM)
    return pl.pallas_call(
        functools.partial(expert_kernel, n_pieces, n_parts, n_ready),
        in_specs=[vmem] * (n_pieces + n_parts + n_ready) + [pl.BlockSpec(memory_space=pltpu.HBM)],
        out_specs=[vmem] * n_pieces,
        out_shape=[pltpu.VMEM((size, width), BF16)] * n_pieces,
        scratch_shapes=[
            pltpu.VMEM((hidden_units, width - sum(early.shape[1] for early in ready)), BF16),
            pltpu.VMEM((rows, width), BF16),
            pltpu.VMEM((rows, hidden_units), BF16),
            pltpu.SemaphoreType.DMA((2,)),
        ],
        compiler_params=pltpu.CompilerParams(vmem_limit_bytes=20 * 2**20),
        name="experts",
    )(*map(in_vmem, [*pieces, *parts, *ready]), in_hbm(down))


def in_vmem(value):
    return pltpu.with_memory_space_constraint(value, pltpu.VMEM)


def in_hbm(value):
    return pltpu.with_memory_space_constraint(value, pltpu.HBM)


def swap(value, axis, bits):
    n = lax.axis_size(axis)
    return lax.ppermute(value, axis, [(i, i ^ bits) for i in range(n)])


def strides(size):
    return [size >> i for i in range(1, size.bit_length())]


def added(*parts):
    total = parts[0].astype(F32)
    for part in parts[1:]:
        total = total + part.astype(F32)
    return total.astype(BF16)


def exchanged(parts, axis, stride):
    half = len(parts) // 2
    return [added(parts[i], swap(parts[half + i], axis, stride)) for i in range(half)]


def shards(
    tokens, queries, stored_keys, stored_values, lengths, norm_gain, routes, route_weights,
    gate_up, down_proj,
):
    resid, row, first_part = attend(
        tokens, queries, stored_keys, stored_values, lengths, norm_gain, routes, route_weights,
        gate_up[0],
    )
    gate_up, down = gate_up[0], down_proj[0]
    two, hidden_units, width = gate_up.shape
    weight_parts, ready = [first_part], []

    def gate_part(first, size):
        return (weight_parts, gate_up, (slice(None), slice(first, first + size)), (two, size, width))

    def down_blocks(first, n):
        wide = width // BLOCKS
        cut = (slice(None), slice(first * wide, (first + n) * wide))
        return (ready, down, cut, (hidden_units, n * wide))

    waiting = []
    if len(spans(hidden_units)) == 3:
        second, third = spans(hidden_units)[1:]
        early, more = EARLY_BLOCKS
        waiting = [
            [down_blocks(0, early)],
            [gate_part(*second)],
            [gate_part(*third), down_blocks(early, more)],
        ]

    def beside(values):
        if not waiting:
            return values
        kept, arrays, cuts, shapes = zip(*waiting.pop(0))
        brought = bring(arrays, cuts, shapes)
        *brought, values = lax.optimization_barrier((*brought, values))
        for where, part in zip(kept, brought):
            where.append(part)
        return values

    tp_steps = strides(lax.axis_size("tp"))
    side_steps = strides(lax.axis_size("side"))
    held = row
    for stride in tp_steps:
        held = join([held, beside(swap(held, "tp", stride))])
    pieces = [held]
    for stride in side_steps:
        pieces = pieces + beside([swap(piece, "side", stride) for piece in pieces])
    while waiting:
        beside(())
    parts = experts(pieces, weight_parts, ready, down)
    for stride in reversed(side_steps):
        half = len(parts) // 2
        parts = [added(parts[i], swap(parts[half + i], "side", stride)) for i in range(half)]
    total = parts[0].astype(F32)
    while tp_steps:
        near, tp_steps = tp_steps[-2:], tp_steps[:-2]
        away = [0]
        for stride in near:
            away = away + [stride ^ k for k in away]
        size = total.shape[0] // len(away)
        sent = total.astype(BF16)
        total = total[:size]
        if not tp_steps:
            total = resid + total
        far_first = sorted(range(1, len(away)), key=lambda i: -away[i])
        for i in far_first:
            total = total + swap(sent[i * size : (i + 1) * size], "tp", away[i]).astype(F32)
    return total.astype(BF16)


def solution(mesh):
    rows = ("groups", "side", "tp")
    placed = (
        P(rows, None),
        P(rows, None),
        P(rows, None, None),
        P(rows, None, None),
        P(rows),
        P(),
        P(rows, None),
        P(rows, None),
        P("side", None, "tp", None),
        P("side", "tp", None),
    )
    return jax.shard_map(
        shards, mesh=mesh, in_specs=placed, out_specs=P(rows, None), check_vma=False
    )
```

```python
import functools
import math

import jax
import jax.numpy as jnp
from jax import lax
from jax.experimental import pallas as pl
from jax.experimental.pallas import tpu as pltpu
from jax.sharding import PartitionSpec as P

HEAD_SIZE = 128
LANES = 128
EARLY_BLOCKS = (3, 1)
BLOCKS = 8
F32 = jnp.float32
BF16 = jnp.bfloat16


def attend_kernel(
    *refs,
):
    small_hbm, (keys_hbm, values_hbm, ahead_hbm) = refs[:6], refs[6:9]
    resid_ref, row_ref, ahead = refs[9:12]
    small, (keys, values) = refs[12:18], refs[18:20]
    small_sems, key_sems, value_sems, ahead_sems = refs[20:]
    queries, tokens, gain, lengths, routes, weights = small
    rows, positions, kv_width = keys_hbm.shape
    width = tokens.shape[1]
    small_copies = [
        pltpu.make_async_copy(source, target, small_sems.at[i])
        for i, (source, target) in enumerate(zip(small_hbm, small))
    ]
    for copy in small_copies:
        copy.start()
    n_kv = kv_width // HEAD_SIZE
    per = width // kv_width
    key_copies = [
        pltpu.make_async_copy(keys_hbm.at[t], keys.at[t], key_sems.at[t]) for t in range(rows)
    ]
    value_copies = [
        pltpu.make_async_copy(values_hbm.at[t], values.at[t], value_sems.at[t])
        for t in range(rows)
    ]
    ahead_copies = ahead_parts(ahead_hbm, ahead, ahead_sems, 0)
    for copy in key_copies + value_copies + ahead_copies:
        copy.start()
    for copy in small_copies:
        copy.wait()
    block = per * rows
    owner = lax.broadcasted_iota(jnp.int32, (block, 1), 0) % rows
    length = jnp.zeros((block, 1), jnp.int32)
    for t in range(rows):
        length = jnp.where(owner == t, lengths[0, t], length)
    alive = lax.broadcasted_iota(jnp.int32, (block, positions), 1) < length
    q = queries[...].astype(F32)
    stacked = []
    for g in range(n_kv):
        heads = [
            q[:, (g * per + j) * HEAD_SIZE : (g * per + j + 1) * HEAD_SIZE] for j in range(per)
        ]
        stacked.append(jnp.concatenate(heads, axis=0))
    for copy in key_copies:
        copy.wait()
    scores = []
    for g in range(n_kv):
        total = jnp.zeros((block, positions), F32)
        for t in range(rows):
            mine = jnp.where(owner == t, stacked[g], 0.0).astype(BF16)
            total += lax.dot_general(
                mine, keys[t, :, g * HEAD_SIZE : (g + 1) * HEAD_SIZE],
                (((1,), (1,)), ((), ())), preferred_element_type=F32,
            )
        scores.append(total)
    probs = []
    for g in range(n_kv):
        s = jnp.where(alive, scores[g] / math.sqrt(HEAD_SIZE), -1e30)
        peak = jnp.max(s, axis=1, keepdims=True)
        e = jnp.where(alive, jnp.exp(s - peak), 0.0)
        probs.append((e / jnp.sum(e, axis=1, keepdims=True)).astype(BF16).astype(F32))
    for copy in value_copies:
        copy.wait()
    squares = jnp.zeros((rows, HEAD_SIZE), F32)
    for g in range(n_kv):
        total = jnp.zeros((block, HEAD_SIZE), F32)
        for t in range(rows):
            mine = jnp.where(owner == t, probs[g], 0.0).astype(BF16)
            total += jnp.dot(
                mine, values[t, :, g * HEAD_SIZE : (g + 1) * HEAD_SIZE],
                preferred_element_type=F32,
            )
        for j in range(per):
            at = slice((g * per + j) * HEAD_SIZE, (g * per + j + 1) * HEAD_SIZE)
            piece = tokens[:, at].astype(F32) + total[j * rows : (j + 1) * rows]
            resid_ref[:, at] = piece
            squares += piece * piece
    mean = jnp.sum(squares, axis=1, keepdims=True) / width
    scale = lax.rsqrt(mean + 1e-05)
    row_ref[:, :width] = (resid_ref[...] * scale * gain[...]).astype(BF16)
    row_at = lax.broadcasted_iota(jnp.int32, (rows, LANES), 0)
    lane = lax.broadcasted_iota(jnp.int32, (rows, LANES), 1)
    high = jnp.zeros((rows, LANES), F32)
    low = jnp.zeros((rows, LANES), F32)
    for t in range(rows):
        for k in range(routes.shape[0]):
            hit = row_at == t
            high += jnp.where(hit & (lane == routes[k, t]), weights[k, t], 0.0)
            low += jnp.where(hit & (lane == routes[k, t] + LANES // 2), weights[k, t], 0.0)
    low = low - low.astype(BF16).astype(F32)
    row_ref[:, width:] = (high.astype(BF16).astype(F32) + low).astype(BF16)
    for copy in ahead_copies:
        copy.wait()


def spans(hidden_units):
    n = 3 if hidden_units > 1024 and hidden_units % 48 == 0 else 1
    size = hidden_units // n
    return [(i * size, size) for i in range(n)]


def ahead_parts(source, target, sems, first):
    size = target.shape[1]
    return [
        pltpu.make_async_copy(source.at[i, first : first + size], target.at[i], sems.at[i])
        for i in range(2)
    ]


def ahead_shape(gate_up, part):
    two, hidden_units, width = gate_up.shape
    return pltpu.VMEM((two, spans(hidden_units)[part][1], width), gate_up.dtype)


def bring_kernel(cuts, *refs):
    n = len(cuts)
    sources, targets, sems = refs[:n], refs[n : 2 * n], refs[2 * n]
    copies = [
        pltpu.make_async_copy(sources[i].at[cut], targets[i], sems.at[i])
        for i, cut in enumerate(cuts)
    ]
    for copy in copies:
        copy.start()
    for copy in copies:
        copy.wait()


def bring(arrays, cuts, shapes):
    n = len(arrays)
    return pl.pallas_call(
        functools.partial(bring_kernel, cuts),
        in_specs=[pl.BlockSpec(memory_space=pltpu.HBM)] * n,
        out_specs=[pl.BlockSpec(memory_space=pltpu.VMEM)] * n,
        out_shape=[pltpu.VMEM(shape, BF16) for shape in shapes],
        scratch_shapes=[pltpu.SemaphoreType.DMA((n,))],
        cost_estimate=pl.CostEstimate(
            flops=0, transcendentals=0, bytes_accessed=2 * sum(map(math.prod, shapes))
        ),
        compiler_params=pltpu.CompilerParams(vmem_limit_bytes=2**20),
        name="bring",
    )(*map(in_hbm, arrays))


def attend(tokens, queries, keys, values, lengths, gain, routes, weights, gate_up):
    rows, width = tokens.shape
    vmem = pl.BlockSpec(memory_space=pltpu.VMEM)
    operands = [
        queries, tokens, gain.reshape(1, width), lengths.reshape(1, rows), routes.T, weights.T,
        keys, values, gate_up,
    ]
    return pl.pallas_call(
        attend_kernel,
        in_specs=[pl.BlockSpec(memory_space=pltpu.HBM)] * len(operands),
        out_specs=[vmem, vmem, vmem],
        out_shape=[
            pltpu.VMEM((rows, width), F32),
            pltpu.VMEM((rows, width + LANES), BF16),
            ahead_shape(gate_up, 0),
        ],
        scratch_shapes=[
            pltpu.VMEM(queries.shape, BF16),
            pltpu.VMEM(tokens.shape, BF16),
            pltpu.VMEM((1, width), F32),
            pltpu.SMEM((1, rows), jnp.int32),
            pltpu.SMEM((routes.shape[1], rows), jnp.int32),
            pltpu.SMEM((routes.shape[1], rows), F32),
            pltpu.VMEM(keys.shape, BF16),
            pltpu.VMEM(values.shape, BF16),
            pltpu.SemaphoreType.DMA((6,)),
            pltpu.SemaphoreType.DMA((rows,)),
            pltpu.SemaphoreType.DMA((rows,)),
            pltpu.SemaphoreType.DMA((2,)),
        ],
        compiler_params=pltpu.CompilerParams(vmem_limit_bytes=12 * 2**20),
        name="attend",
    )(*map(in_hbm, operands))


def expert_kernel(n_pieces, n_parts, n_ready, *refs):
    expert = lax.axis_index("side").astype(jnp.int32)
    refs = list(refs)

    def take(n):
        taken, refs[:n] = refs[:n], []
        return taken

    pieces, parts, ready, (down_hbm,) = take(n_pieces), take(n_parts), take(n_ready), take(1)
    outs, (loaded, x, hidden, down_sems) = take(n_pieces), take(4)
    width = x.shape[1]
    wide = width // BLOCKS
    skip = width - loaded.shape[1]
    down_copies = [
        pltpu.make_async_copy(
            down_hbm.at[:, skip + c * wide : skip + (c + 1) * wide],
            loaded.at[:, c * wide : (c + 1) * wide],
            down_sems.at[c],
        )
        for c in range(loaded.shape[1] // wide)
    ]
    at_head = len(down_copies) // 2
    for copy in down_copies[:at_head]:
        copy.start()
    size = pieces[0].shape[0]
    factors = []
    for i in range(n_pieces):
        at = slice(i * size, (i + 1) * size)
        x[at] = pieces[i][:, :width]
        meta = pieces[i][:, width:].astype(F32)
        lane = lax.broadcasted_iota(jnp.int32, meta.shape, 1)
        mine = lane % (LANES // 2) == expert
        factors.append(jnp.sum(jnp.where(mine, meta, 0.0), axis=1, keepdims=True))
    first = 0
    for part in parts:
        units = part.shape[1]
        gate, up = [
            lax.dot_general(
                x[...], part[i], (((1,), (1,)), ((), ())), preferred_element_type=F32
            )
            for i in range(2)
        ]
        hidden[:, first : first + units] = (gate / (1.0 + jnp.exp(-gate)) * up).astype(BF16)
        first += units
        if part is parts[0]:
            for copy in down_copies[at_head:]:
                copy.start()
    first = 0
    for down in ready + [loaded]:
        for c in range(down.shape[1] // wide):
            if down is loaded:
                down_copies[c].wait()
            block = down[:, c * wide : (c + 1) * wide]
            total = jnp.dot(hidden[...], block, preferred_element_type=F32)
            for i, out in enumerate(outs):
                part = total[i * size : (i + 1) * size] * factors[i]
                out[:, first : first + wide] = part.astype(BF16)
            first += wide


def join_kernel(*refs):
    out = refs[-1]
    out[...] = jnp.concatenate([ref[...].astype(F32) for ref in refs[:-1]], axis=0).astype(BF16)


def join(pieces):
    size, width = pieces[0].shape
    vmem = pl.BlockSpec(memory_space=pltpu.VMEM)
    return pl.pallas_call(
        join_kernel,
        in_specs=[vmem] * len(pieces),
        out_specs=vmem,
        out_shape=pltpu.VMEM((len(pieces) * size, width), BF16),
        compiler_params=pltpu.CompilerParams(vmem_limit_bytes=2 * 2**20),
        name="join",
    )(*map(in_vmem, pieces))


def experts(pieces, parts, ready, down):
    n_pieces, n_parts, n_ready = len(pieces), len(parts), len(ready)
    size, width = pieces[0].shape[0], pieces[0].shape[1] - LANES
    hidden_units = down.shape[0]
    rows = n_pieces * size
    vmem = pl.BlockSpec(memory_space=pltpu.VMEM)
    return pl.pallas_call(
        functools.partial(expert_kernel, n_pieces, n_parts, n_ready),
        in_specs=[vmem] * (n_pieces + n_parts + n_ready) + [pl.BlockSpec(memory_space=pltpu.HBM)],
        out_specs=[vmem] * n_pieces,
        out_shape=[pltpu.VMEM((size, width), BF16)] * n_pieces,
        scratch_shapes=[
            pltpu.VMEM((hidden_units, width - sum(early.shape[1] for early in ready)), BF16),
            pltpu.VMEM((rows, width), BF16),
            pltpu.VMEM((rows, hidden_units), BF16),
            pltpu.SemaphoreType.DMA((BLOCKS,)),
        ],
        compiler_params=pltpu.CompilerParams(vmem_limit_bytes=20 * 2**20),
        name="experts",
    )(*map(in_vmem, [*pieces, *parts, *ready]), in_hbm(down))


def in_vmem(value):
    return pltpu.with_memory_space_constraint(value, pltpu.VMEM)


def in_hbm(value):
    return pltpu.with_memory_space_constraint(value, pltpu.HBM)


def swap(value, axis, bits):
    n = lax.axis_size(axis)
    return lax.ppermute(value, axis, [(i, i ^ bits) for i in range(n)])


def strides(size):
    return [size >> i for i in range(1, size.bit_length())]


def added(*parts):
    total = parts[0].astype(F32)
    for part in parts[1:]:
        total = total + part.astype(F32)
    return total.astype(BF16)


def exchanged(parts, axis, stride):
    half = len(parts) // 2
    return [added(parts[i], swap(parts[half + i], axis, stride)) for i in range(half)]


def shards(
    tokens, queries, stored_keys, stored_values, lengths, norm_gain, routes, route_weights,
    gate_up, down_proj,
):
    resid, row, first_part = attend(
        tokens, queries, stored_keys, stored_values, lengths, norm_gain, routes, route_weights,
        gate_up[0],
    )
    gate_up, down = gate_up[0], down_proj[0]
    two, hidden_units, width = gate_up.shape
    weight_parts, ready = [first_part], []

    def gate_part(first, size):
        return (weight_parts, gate_up, (slice(None), slice(first, first + size)), (two, size, width))

    def down_blocks(first, n):
        wide = width // BLOCKS
        cut = (slice(None), slice(first * wide, (first + n) * wide))
        return (ready, down, cut, (hidden_units, n * wide))

    waiting = []
    if len(spans(hidden_units)) == 3:
        second, third = spans(hidden_units)[1:]
        early, more = EARLY_BLOCKS
        waiting = [
            [down_blocks(0, early)],
            [gate_part(*second)],
            [gate_part(*third), down_blocks(early, more)],
        ]

    def beside(values):
        if not waiting:
            return values
        kept, arrays, cuts, shapes = zip(*waiting.pop(0))
        brought = bring(arrays, cuts, shapes)
        *brought, values = lax.optimization_barrier((*brought, values))
        for where, part in zip(kept, brought):
            where.append(part)
        return values

    tp_steps = strides(lax.axis_size("tp"))
    side_steps = strides(lax.axis_size("side"))
    held = row
    for stride in tp_steps:
        held = join([held, beside(swap(held, "tp", stride))])
    pieces = [held]
    for stride in side_steps:
        pieces = pieces + beside([swap(piece, "side", stride) for piece in pieces])
    while waiting:
        beside(())
    parts = experts(pieces, weight_parts, ready, down)
    for stride in reversed(side_steps[1:]):
        half = len(parts) // 2
        parts = [added(parts[i], swap(parts[half + i], "side", stride)) for i in range(half)]
    blocks = 4 if len(tp_steps) > 1 else 2
    near, far = [part.reshape(blocks, part.shape[0] // blocks, width) for part in parts]
    moving = added(near[1:], swap(far[1:], "side", side_steps[0]))
    moving, staying = lax.optimization_barrier((moving, far[0]))
    sent = [None] + [moving[i] for i in range(blocks - 1)]
    total = near[0].astype(F32) + swap(staying, "side", side_steps[0]).astype(F32)
    while tp_steps:
        steps, tp_steps = tp_steps[-2:], tp_steps[:-2]
        away = [0]
        for stride in steps:
            away = away + [stride ^ k for k in away]
        if sent is None:
            size = total.shape[0] // len(away)
            whole = total.astype(BF16)
            sent = [whole[i * size : (i + 1) * size] for i in range(len(away))]
            total = total[:size]
        if not tp_steps:
            total = resid + total
        for i in sorted(range(1, len(away)), key=lambda i: -away[i]):
            total = total + swap(sent[i], "tp", away[i]).astype(F32)
        sent = None
    return total.astype(BF16)


def solution(mesh):
    rows = ("groups", "side", "tp")
    placed = (
        P(rows, None),
        P(rows, None),
        P(rows, None, None),
        P(rows, None, None),
        P(rows),
        P(),
        P(rows, None),
        P(rows, None),
        P("side", None, "tp", None),
        P("side", "tp", None),
    )
    return jax.shard_map(
        shards, mesh=mesh, in_specs=placed, out_specs=P(rows, None), check_vma=False
    )
```

```python
import functools
import math

import jax
import jax.numpy as jnp
from jax import lax
from jax.experimental import pallas as pl
from jax.experimental.pallas import tpu as pltpu
from jax.sharding import PartitionSpec as P

HEAD_SIZE = 128
LANES = 128
EARLY_BLOCKS = (1, 1)
BLOCKS = 8
F32 = jnp.float32
BF16 = jnp.bfloat16


def attend_kernel(
    *refs,
):
    small_hbm, (keys_hbm, values_hbm, ahead_hbm) = refs[:6], refs[6:9]
    resid_ref, row_ref, ahead = refs[9:12]
    small, (keys, values) = refs[12:18], refs[18:20]
    small_sems, key_sems, value_sems, ahead_sems = refs[20:]
    queries, tokens, gain, lengths, routes, weights = small
    rows, positions, kv_width = keys_hbm.shape
    width = tokens.shape[1]
    small_copies = [
        pltpu.make_async_copy(source, target, small_sems.at[i])
        for i, (source, target) in enumerate(zip(small_hbm, small))
    ]
    for copy in small_copies:
        copy.start()
    n_kv = kv_width // HEAD_SIZE
    per = width // kv_width
    key_copies = [
        pltpu.make_async_copy(keys_hbm.at[t], keys.at[t], key_sems.at[t]) for t in range(rows)
    ]
    value_copies = [
        pltpu.make_async_copy(values_hbm.at[t], values.at[t], value_sems.at[t])
        for t in range(rows)
    ]
    ahead_copies = ahead_parts(ahead_hbm, ahead, ahead_sems, 0)
    for copy in key_copies + value_copies + ahead_copies:
        copy.start()
    for copy in small_copies:
        copy.wait()
    block = per * rows
    owner = lax.broadcasted_iota(jnp.int32, (block, 1), 0) % rows
    length = jnp.zeros((block, 1), jnp.int32)
    for t in range(rows):
        length = jnp.where(owner == t, lengths[0, t], length)
    alive = lax.broadcasted_iota(jnp.int32, (block, positions), 1) < length
    q = queries[...].astype(F32)
    stacked = []
    for g in range(n_kv):
        heads = [
            q[:, (g * per + j) * HEAD_SIZE : (g * per + j + 1) * HEAD_SIZE] for j in range(per)
        ]
        stacked.append(jnp.concatenate(heads, axis=0))
    for copy in key_copies:
        copy.wait()
    scores = []
    for g in range(n_kv):
        total = jnp.zeros((block, positions), F32)
        for t in range(rows):
            mine = jnp.where(owner == t, stacked[g], 0.0).astype(BF16)
            total += lax.dot_general(
                mine, keys[t, :, g * HEAD_SIZE : (g + 1) * HEAD_SIZE],
                (((1,), (1,)), ((), ())), preferred_element_type=F32,
            )
        scores.append(total)
    probs = []
    for g in range(n_kv):
        s = jnp.where(alive, scores[g] / math.sqrt(HEAD_SIZE), -1e30)
        peak = jnp.max(s, axis=1, keepdims=True)
        e = jnp.where(alive, jnp.exp(s - peak), 0.0)
        probs.append((e / jnp.sum(e, axis=1, keepdims=True)).astype(BF16).astype(F32))
    for copy in value_copies:
        copy.wait()
    squares = jnp.zeros((rows, HEAD_SIZE), F32)
    for g in range(n_kv):
        total = jnp.zeros((block, HEAD_SIZE), F32)
        for t in range(rows):
            mine = jnp.where(owner == t, probs[g], 0.0).astype(BF16)
            total += jnp.dot(
                mine, values[t, :, g * HEAD_SIZE : (g + 1) * HEAD_SIZE],
                preferred_element_type=F32,
            )
        for j in range(per):
            at = slice((g * per + j) * HEAD_SIZE, (g * per + j + 1) * HEAD_SIZE)
            piece = tokens[:, at].astype(F32) + total[j * rows : (j + 1) * rows]
            resid_ref[:, at] = piece
            squares += piece * piece
    mean = jnp.sum(squares, axis=1, keepdims=True) / width
    scale = lax.rsqrt(mean + 1e-05)
    row_ref[:, :width] = (resid_ref[...] * scale * gain[...]).astype(BF16)
    row_at = lax.broadcasted_iota(jnp.int32, (rows, LANES), 0)
    lane = lax.broadcasted_iota(jnp.int32, (rows, LANES), 1)
    high = jnp.zeros((rows, LANES), F32)
    low = jnp.zeros((rows, LANES), F32)
    for t in range(rows):
        for k in range(routes.shape[0]):
            hit = row_at == t
            high += jnp.where(hit & (lane == routes[k, t]), weights[k, t], 0.0)
            low += jnp.where(hit & (lane == routes[k, t] + LANES // 2), weights[k, t], 0.0)
    low = low - low.astype(BF16).astype(F32)
    row_ref[:, width:] = (high.astype(BF16).astype(F32) + low).astype(BF16)
    for copy in ahead_copies:
        copy.wait()


def spans(hidden_units):
    n = 3 if hidden_units > 1024 and hidden_units % 48 == 0 else 1
    size = hidden_units // n
    return [(i * size, size) for i in range(n)]


def ahead_parts(source, target, sems, first):
    size = target.shape[1]
    return [
        pltpu.make_async_copy(source.at[i, first : first + size], target.at[i], sems.at[i])
        for i in range(2)
    ]


def ahead_shape(gate_up, part):
    two, hidden_units, width = gate_up.shape
    return pltpu.VMEM((two, spans(hidden_units)[part][1], width), gate_up.dtype)


def bring_kernel(cuts, *refs):
    n = len(cuts)
    sources, targets, sems = refs[:n], refs[n : 2 * n], refs[2 * n]
    copies = [
        pltpu.make_async_copy(sources[i].at[cut], targets[i], sems.at[i])
        for i, cut in enumerate(cuts)
    ]
    for copy in copies:
        copy.start()
    for copy in copies:
        copy.wait()


def bring(arrays, cuts, shapes):
    n = len(arrays)
    return pl.pallas_call(
        functools.partial(bring_kernel, cuts),
        in_specs=[pl.BlockSpec(memory_space=pltpu.HBM)] * n,
        out_specs=[pl.BlockSpec(memory_space=pltpu.VMEM)] * n,
        out_shape=[pltpu.VMEM(shape, BF16) for shape in shapes],
        scratch_shapes=[pltpu.SemaphoreType.DMA((n,))],
        cost_estimate=pl.CostEstimate(
            flops=0, transcendentals=0, bytes_accessed=2 * sum(map(math.prod, shapes))
        ),
        compiler_params=pltpu.CompilerParams(vmem_limit_bytes=2**20),
        name="bring",
    )(*map(in_hbm, arrays))


def attend(tokens, queries, keys, values, lengths, gain, routes, weights, gate_up):
    rows, width = tokens.shape
    vmem = pl.BlockSpec(memory_space=pltpu.VMEM)
    operands = [
        queries, tokens, gain.reshape(1, width), lengths.reshape(1, rows), routes.T, weights.T,
        keys, values, gate_up,
    ]
    return pl.pallas_call(
        attend_kernel,
        in_specs=[pl.BlockSpec(memory_space=pltpu.HBM)] * len(operands),
        out_specs=[vmem, vmem, vmem],
        out_shape=[
            pltpu.VMEM((rows, width), F32),
            pltpu.VMEM((rows, width + LANES), BF16),
            ahead_shape(gate_up, 0),
        ],
        scratch_shapes=[
            pltpu.VMEM(queries.shape, BF16),
            pltpu.VMEM(tokens.shape, BF16),
            pltpu.VMEM((1, width), F32),
            pltpu.SMEM((1, rows), jnp.int32),
            pltpu.SMEM((routes.shape[1], rows), jnp.int32),
            pltpu.SMEM((routes.shape[1], rows), F32),
            pltpu.VMEM(keys.shape, BF16),
            pltpu.VMEM(values.shape, BF16),
            pltpu.SemaphoreType.DMA((6,)),
            pltpu.SemaphoreType.DMA((rows,)),
            pltpu.SemaphoreType.DMA((rows,)),
            pltpu.SemaphoreType.DMA((2,)),
        ],
        compiler_params=pltpu.CompilerParams(vmem_limit_bytes=12 * 2**20),
        name="attend",
    )(*map(in_hbm, operands))


def expert_kernel(n_pieces, n_parts, n_ready, *refs):
    expert = lax.axis_index("side").astype(jnp.int32)
    refs = list(refs)

    def take(n):
        taken, refs[:n] = refs[:n], []
        return taken

    pieces, parts, ready, (down_hbm,) = take(n_pieces), take(n_parts), take(n_ready), take(1)
    outs, (loaded, x, hidden, down_sems) = take(n_pieces), take(4)
    width = x.shape[1]
    wide = width // BLOCKS
    skip = width - loaded.shape[1]
    down_copies = [
        pltpu.make_async_copy(
            down_hbm.at[:, skip + c * wide : skip + (c + 1) * wide],
            loaded.at[:, c * wide : (c + 1) * wide],
            down_sems.at[c],
        )
        for c in range(loaded.shape[1] // wide)
    ]
    at_head = len(down_copies) // 2
    for copy in down_copies[:at_head]:
        copy.start()
    size = pieces[0].shape[0]
    factors = []
    for i in range(n_pieces):
        at = slice(i * size, (i + 1) * size)
        x[at] = pieces[i][:, :width]
        meta = pieces[i][:, width:].astype(F32)
        lane = lax.broadcasted_iota(jnp.int32, meta.shape, 1)
        mine = lane % (LANES // 2) == expert
        factors.append(jnp.sum(jnp.where(mine, meta, 0.0), axis=1, keepdims=True))
    first = 0
    for part in parts:
        units = part.shape[1]
        gate, up = [
            lax.dot_general(
                x[...], part[i], (((1,), (1,)), ((), ())), preferred_element_type=F32
            )
            for i in range(2)
        ]
        hidden[:, first : first + units] = (gate / (1.0 + jnp.exp(-gate)) * up).astype(BF16)
        first += units
        if part is parts[0]:
            for copy in down_copies[at_head:]:
                copy.start()
    first = 0
    for down in ready + [loaded]:
        for c in range(down.shape[1] // wide):
            if down is loaded:
                down_copies[c].wait()
            block = down[:, c * wide : (c + 1) * wide]
            total = jnp.dot(hidden[...], block, preferred_element_type=F32)
            for i, out in enumerate(outs):
                part = total[i * size : (i + 1) * size] * factors[i]
                out[:, first : first + wide] = part.astype(BF16)
            first += wide


def join_kernel(*refs):
    out = refs[-1]
    out[...] = jnp.concatenate([ref[...].astype(F32) for ref in refs[:-1]], axis=0).astype(BF16)


def join(pieces):
    size, width = pieces[0].shape
    vmem = pl.BlockSpec(memory_space=pltpu.VMEM)
    return pl.pallas_call(
        join_kernel,
        in_specs=[vmem] * len(pieces),
        out_specs=vmem,
        out_shape=pltpu.VMEM((len(pieces) * size, width), BF16),
        compiler_params=pltpu.CompilerParams(vmem_limit_bytes=2 * 2**20),
        name="join",
    )(*map(in_vmem, pieces))


def experts(pieces, parts, ready, down):
    n_pieces, n_parts, n_ready = len(pieces), len(parts), len(ready)
    size, width = pieces[0].shape[0], pieces[0].shape[1] - LANES
    hidden_units = down.shape[0]
    rows = n_pieces * size
    vmem = pl.BlockSpec(memory_space=pltpu.VMEM)
    return pl.pallas_call(
        functools.partial(expert_kernel, n_pieces, n_parts, n_ready),
        in_specs=[vmem] * (n_pieces + n_parts + n_ready) + [pl.BlockSpec(memory_space=pltpu.HBM)],
        out_specs=[vmem] * n_pieces,
        out_shape=[pltpu.VMEM((size, width), BF16)] * n_pieces,
        scratch_shapes=[
            pltpu.VMEM((hidden_units, width - sum(early.shape[1] for early in ready)), BF16),
            pltpu.VMEM((rows, width), BF16),
            pltpu.VMEM((rows, hidden_units), BF16),
            pltpu.SemaphoreType.DMA((BLOCKS,)),
        ],
        compiler_params=pltpu.CompilerParams(vmem_limit_bytes=20 * 2**20),
        name="experts",
    )(*map(in_vmem, [*pieces, *parts, *ready]), in_hbm(down))


def in_vmem(value):
    return pltpu.with_memory_space_constraint(value, pltpu.VMEM)


def in_hbm(value):
    return pltpu.with_memory_space_constraint(value, pltpu.HBM)


def swap(value, axis, bits):
    n = lax.axis_size(axis)
    return lax.ppermute(value, axis, [(i, i ^ bits) for i in range(n)])


def strides(size):
    return [size >> i for i in range(1, size.bit_length())]


def added(*parts):
    total = parts[0].astype(F32)
    for part in parts[1:]:
        total = total + part.astype(F32)
    return total.astype(BF16)


def exchanged(parts, axis, stride):
    half = len(parts) // 2
    return [added(parts[i], swap(parts[half + i], axis, stride)) for i in range(half)]


def shards(
    tokens, queries, stored_keys, stored_values, lengths, norm_gain, routes, route_weights,
    gate_up, down_proj,
):
    resid, row, first_part = attend(
        tokens, queries, stored_keys, stored_values, lengths, norm_gain, routes, route_weights,
        gate_up[0],
    )
    gate_up, down = gate_up[0], down_proj[0]
    two, hidden_units, width = gate_up.shape
    weight_parts, ready = [first_part], []

    def gate_part(first, size):
        return (weight_parts, gate_up, (slice(None), slice(first, first + size)), (two, size, width))

    def down_blocks(first, n):
        wide = width // BLOCKS
        cut = (slice(None), slice(first * wide, (first + n) * wide))
        return (ready, down, cut, (hidden_units, n * wide))

    waiting = []
    if len(spans(hidden_units)) == 3:
        second, third = spans(hidden_units)[1:]
        early, more = EARLY_BLOCKS
        waiting = [
            [gate_part(*second), down_blocks(0, early)],
            [gate_part(*third), down_blocks(early, more)],
        ]

    def beside(values):
        if not waiting:
            return values
        kept, arrays, cuts, shapes = zip(*waiting.pop(0))
        brought = bring(arrays, cuts, shapes)
        *brought, values = lax.optimization_barrier((*brought, values))
        for where, part in zip(kept, brought):
            where.append(part)
        return values

    tp_steps = strides(lax.axis_size("tp"))
    side_steps = strides(lax.axis_size("side"))
    held = row
    for steps in [tp_steps[i : i + 2] for i in range(0, len(tp_steps), 2)]:
        away = [0]
        for stride in steps:
            away = away + [stride ^ k for k in away]
        far_first = sorted(range(1, len(away)), key=lambda i: -away[i])
        got = beside([swap(held, "tp", away[i]) for i in far_first])
        held = join([held] + [got[far_first.index(i)] for i in range(1, len(away))])
    pieces = [held]
    for stride in side_steps:
        pieces = pieces + beside([swap(piece, "side", stride) for piece in pieces])
    while waiting:
        beside(())
    parts = experts(pieces, weight_parts, ready, down)
    for stride in reversed(side_steps[1:]):
        half = len(parts) // 2
        parts = [added(parts[i], swap(parts[half + i], "side", stride)) for i in range(half)]
    blocks = 4 if len(tp_steps) > 1 else 2
    near, far = [part.reshape(blocks, part.shape[0] // blocks, width) for part in parts]
    moving = added(near[1:], swap(far[1:], "side", side_steps[0]))
    moving, staying = lax.optimization_barrier((moving, far[0]))
    sent = [None] + [moving[i] for i in range(blocks - 1)]
    total = near[0].astype(F32) + swap(staying, "side", side_steps[0]).astype(F32)
    while tp_steps:
        steps, tp_steps = tp_steps[-2:], tp_steps[:-2]
        away = [0]
        for stride in steps:
            away = away + [stride ^ k for k in away]
        if sent is None:
            size = total.shape[0] // len(away)
            whole = total.astype(BF16)
            sent = [whole[i * size : (i + 1) * size] for i in range(len(away))]
            total = total[:size]
        if not tp_steps:
            total = resid + total
        for i in sorted(range(1, len(away)), key=lambda i: -away[i]):
            total = total + swap(sent[i], "tp", away[i]).astype(F32)
        sent = None
    return total.astype(BF16)


def solution(mesh):
    rows = ("groups", "side", "tp")
    placed = (
        P(rows, None),
        P(rows, None),
        P(rows, None, None),
        P(rows, None, None),
        P(rows),
        P(),
        P(rows, None),
        P(rows, None),
        P("side", None, "tp", None),
        P("side", "tp", None),
    )
    return jax.shard_map(
        shards, mesh=mesh, in_specs=placed, out_specs=P(rows, None), check_vma=False
    )
```
